512 devices in a mesh: gx: 8 (over y), gy: 8 (over x, core), gz: 8 (over z).
Axes of the slice: x: 4, y: 8, z: 8, core: 2. Of those that a mesh axis runs over, the one named last changes fastest.
Arguments:
- positions: float32 [2, 48, 1024, 1024], P(None, 'gz', 'gy', 'gx'), may hold values from -1.2 to 1.2
- velocities: float32 [2, 48, 1024, 1024], P(None, 'gz', 'gy', 'gx'), may hold values from -18 to 18, as said below
- link_codes: int32 [48, 1024, 1024], P('gz', 'gy', 'gx'), may hold values from 0 to 4095, as said below
- fixed_nodes: int32 [48, 1024, 1024], P('gz', 'gy', 'gx'), may hold values 0 or 1
Outputs:
- final_positions: float32 [2, 48, 1024, 1024], P(None, 'gz', 'gy', 'gx')
- final_velocities: float32 [2, 48, 1024, 1024], P(None, 'gz', 'gy', 'gx')
The draws below stay inside these ranges and needn't reach their ends.
Inputs may be any that keep to these rules, and one draw needn't show every extreme that they name: `link_codes`: bit b of an entry is set exactly when the node's link b is valid; a link and its reverse link at the neighbour agree, and links that leave the grid are never set. velocities are finite.
All inputs are finite; a program needn't handle non-finite values. No bound on the sum of `fixed_nodes` on one device may be relied on, other than what follows from the above.
Results may differ from the reference program's by a relative error of at most 0.0001.
Values sent between devices are 32-bit elements; how exact they have to be, the bound alone decides.
A program may use at most 64 MiB of HBM per device.

```python
import math
import jax
import jax.numpy as jnp

ITERS = 3
NX = 1024
NY = 1024
NZ = 48


def shift_back(values, off_z, off_y, off_x):
    padded = jnp.pad(values, 2)
    return padded[2 - off_z:2 - off_z + NZ, 2 - off_y:2 - off_y + NY, 2 - off_x:2 - off_x + NX]


def draw_link_codes(key, part):
    key = jax.random.fold_in(key, 11)
    z = jnp.arange(NZ, dtype=jnp.int32)[:, None, None]
    y = jnp.arange(NY, dtype=jnp.int32)[None, :, None]
    x = jnp.arange(NX, dtype=jnp.int32)[None, None, :]
    pairs = [((0, 0, 1), 0, 1), ((0, 1, 0), 2, 3), ((0, 1, 1), 4, 5), ((0, 1, -1), 6, 7), ((1, 0, 0), 8, 9), ((2, 0, 0), 10, 11)]
    codes = jnp.zeros((NZ, NY, NX), jnp.int32)
    for pair_index, (offset, forward, backward) in enumerate(pairs):
        off_z, off_y, off_x = offset
        inside = (z + off_z >= 0) & (z + off_z < NZ) & (y + off_y >= 0) & (y + off_y < NY) & (x + off_x >= 0) & (x + off_x < NX)
        coins = jax.random.randint(jax.random.fold_in(key, pair_index), (NZ, NY, NX), 0, 10)
        outward = ((coins < 9) & inside).astype(jnp.int32)
        reverse = shift_back(outward, off_z, off_y, off_x)
        codes = codes + outward * (1 << forward) + reverse * (1 << backward)
    return codes


def draw_velocities(key, part):
    key = jax.random.fold_in(key, 12)
    first, second = jax.random.split(key)
    ramp = 1.0 + 2.0 * jnp.arange(NZ, dtype=jnp.float32)[None, :, None, None] / max(NZ - 1, 1)
    rough = jax.random.uniform(second, (2, NZ, NY, NX), jnp.float32, 0.5, 1.5)
    base = jnp.clip(jax.random.normal(first, (2, NZ, NY, NX), jnp.float32), -4.0, 4.0)
    return (base * ramp * rough).astype(jnp.float32)


def plant(array, rng, smallest, top_value):
    dims = array.shape
    place = [jax.random.randint(jax.random.fold_in(rng, axis), (), 0, dims[axis]) for axis in range(len(dims))]
    array = array.at[tuple(place)].set(smallest)
    longest = dims.index(max(dims))
    place[longest] = (place[longest] + 1) % dims[longest]
    return array.at[tuple(place)].set(top_value)


def block_scale(stream_key, dims, shards, low, top_value):
    def one(dim, shards_of):
        steps = jax.random.uniform(jax.random.fold_in(jax.random.fold_in(stream_key, 6), dim), (shards_of,), jnp.float32, low / len(shards), top_value / len(shards))
        return jnp.repeat(jnp.exp(steps), dims[dim] // shards_of).reshape((-1,) + (1,) * (len(dims) - dim - 1))

    factor_of = one(*shards[0])
    for cut in shards[1:]:
        factor_of = factor_of * one(*cut)
    return factor_of


def centred(rng, dims, deviation, bound, shards=(), kind=jnp.bfloat16):
    drawn = deviation * jax.random.normal(rng, dims, jnp.float32)
    if shards:
        drawn = drawn * block_scale(rng, dims, shards, -0.22, 0.18)
    return jnp.clip(drawn, -bound, bound).astype(kind)


def setup_inputs(seed: int = 0) -> dict:
    splits = jax.random.split(jax.random.key(seed), 5)
    positions = centred(splits[0], (2, NZ, NY, NX), 0.3, 1.2, ((1, 8), (2, 8), (3, 8)), jnp.float32)
    velocities = draw_velocities(jax.random.fold_in(splits[4], 71), 0)
    link_codes = draw_link_codes(jax.random.fold_in(splits[4], 71), 0)
    fixed_nodes = plant((jax.random.randint(splits[3], (NZ, NY, NX), 0, 16) < 1).astype(jnp.int32), jax.random.fold_in(splits[3], 1), 0, 1)
    return {"positions": positions, "velocities": velocities, "link_codes": link_codes, "fixed_nodes": fixed_nodes}


PLANE_LINKS = [(0, 1), (0, -1), (1, 0), (-1, 0), (1, 1), (-1, -1), (1, -1), (-1, 1)]
DEPTH_LINKS = [(1, 0.5), (-1, 0.5), (2, 0.25), (-2, 0.25)]
TIME_STEP = 0.3
DAMPING = 0.9
STIFF_PLANE = 1.0
HUBER_DELTA = 0.5
LENGTH_FLOOR = 0.25
ENERGY_CAP = 0.04
EPSILON = 1e-06

def spring_force(center, plane_ext, depth_ext, links):
    depth, rows, cols = (center.shape[1], center.shape[2], center.shape[3])
    force_y = jnp.zeros(center.shape[1:], jnp.float32)
    force_x = jnp.zeros(center.shape[1:], jnp.float32)
    for bit_index, (off_y, off_x) in enumerate(PLANE_LINKS):
        neighbour = plane_ext[:, :, 1 + off_y:1 + off_y + rows, 1 + off_x:1 + off_x + cols]
        delta_y = off_y + neighbour[0] - center[0]
        delta_x = off_x + neighbour[1] - center[1]
        length = jnp.sqrt(delta_y * delta_y + delta_x * delta_x)
        rest_len = math.sqrt(off_y * off_y + off_x * off_x)
        active = (links >> bit_index & 1).astype(jnp.float32)
        magnitude = active * STIFF_PLANE * jnp.clip(length - rest_len, -HUBER_DELTA, HUBER_DELTA) / jnp.maximum(length, LENGTH_FLOOR)
        force_y = force_y + magnitude * delta_y
        force_x = force_x + magnitude * delta_x
    for link_index, (off_z, stiffness) in enumerate(DEPTH_LINKS):
        neighbour = depth_ext[:, 2 + off_z:2 + off_z + depth]
        delta_y = neighbour[0] - center[0]
        delta_x = neighbour[1] - center[1]
        length = jnp.sqrt(delta_y * delta_y + delta_x * delta_x)
        active = (links >> 8 + link_index & 1).astype(jnp.float32)
        magnitude = active * stiffness * HUBER_DELTA / jnp.maximum(length, HUBER_DELTA)
        force_y = force_y + magnitude * delta_y
        force_x = force_x + magnitude * delta_x
    return jnp.stack([force_y, force_x])

def reference(positions, velocities, link_codes, fixed_nodes):
    movable = (1 - fixed_nodes).astype(jnp.float32)
    position = positions
    velocity = velocities
    capacity = ENERGY_CAP * NZ * NY * NX
    for iteration in range(ITERS):
        plane_ext = jnp.pad(position, ((0, 0), (0, 0), (1, 1), (1, 1)))
        depth_ext = jnp.pad(position, ((0, 0), (2, 2), (0, 0), (0, 0)))
        force = spring_force(position, plane_ext, depth_ext, link_codes)
        kicked = (DAMPING * velocity + TIME_STEP * force) * movable
        kinetic = 0.5 * jnp.sum(kicked * kicked)
        factor = jnp.minimum(1.0, jnp.sqrt(capacity / (kinetic + EPSILON)))
        velocity = factor * kicked
        position = position + TIME_STEP * velocity
    return (position, velocity)
```

```python
import functools
import itertools
import math

import jax
import jax.numpy as jnp
from jax import lax
from jax.experimental import pallas as pl
from jax.experimental.pallas import tpu as pltpu
from jax.sharding import PartitionSpec as P

MESH = pl.DeviceIdType.MESH
ITERS = 3
TIME_STEP = 0.3
DAMPING = 0.9
STIFF_PLANE = 1.0
HUBER_DELTA = 0.5
LENGTH_FLOOR = 0.25
ENERGY_CAP = 0.04
EPSILON = 1e-06
DIAG = math.sqrt(2.0)
AXES = ("gx", "gy", "gz")
F32 = jnp.float32

COLUMN_PEERS = ((1, 0), (-1, 0), (1, 1), (-1, 1), (1, -1), (-1, -1))
FROM_LEFT, FROM_RIGHT, FROM_UP_LEFT, FROM_UP_RIGHT, FROM_DOWN_LEFT, FROM_DOWN_RIGHT = range(6)


def lanes_left(a):
    return pltpu.roll(a, 127, 1)


def lanes_right(a):
    return pltpu.roll(a, 1, 1)


def plane_weight(dy, dx, rest, mask):
    square = dy * dy + dx * dx
    u = jnp.minimum(lax.rsqrt(square), 1.0 / LENGTH_FLOOR)
    stretch = jnp.clip(square * u - rest, -HUBER_DELTA, HUBER_DELTA)
    return stretch * u * mask


def depth_weight(dy, dx, mask):
    square = dy * dy + dx * dx
    return jnp.minimum(lax.rsqrt(square), 1.0 / HUBER_DELTA) * mask


def bit(codes, index, scale):
    return jnp.where((codes & (1 << index)) != 0, F32(scale), F32(0.0))


def kernel(sizes, comm, *refs):
    (pos_in, vel_in, code_in, fix_in, pos_out, kick_out, fac_out,
     pos, rolled, kick, force, below, below_right, codes, fixed, m_plane, m_one, m_two, mov,
     z_in, edge_own, edge_in, row_own, row_in, edge_pos, edge_halo, row_pos, up_pos, down_pos,
     m_edge, m_top, edge_force, sum_src, sum_a, sum_b,
     load_sem, out_sem, halo_send, halo_recv, sum_send, sum_recv) = refs
    nx, ny, nz, nodes_all = sizes
    chips = ny // 2
    me = {a: lax.axis_index(a) for a in AXES}

    def shifted(ox, oy, oz):
        return (lax.rem(me["gx"] + ox + nx, nx), lax.rem(me["gy"] + oy + ny, ny), lax.rem(me["gz"] + oz + nz, nz))

    def by_chip(ox, chip, core, oz):
        gy = me["gy"]
        where = lax.rem(lax.div(gy, 2) + chip, chips) * 2 + lax.rem(lax.rem(gy, 2) + core, 2)
        return (lax.rem(me["gx"] + ox, nx), where, lax.rem(me["gz"] + oz, nz))

    def far(o):
        ox, chip, core, oz = o
        return -(min(ox, nx - ox) + min(chip, chips - chip) + min(oz, nz - oz)) - 0.1 * core

    group_a = sorted([(i, 0, c, 0) for i in range(nx) for c in range(2) if i or c], key=far)
    group_b = sorted([(0, c, 0, k) for c in range(chips) for k in range(nz) if c or k], key=far)

    loads = [
        pltpu.make_async_copy(pos_in, pos.at[:, :, pl.ds(0, 128), :], load_sem.at[0]),
        pltpu.make_async_copy(code_in, codes, load_sem.at[1]),
        pltpu.make_async_copy(vel_in, kick, load_sem.at[2]),
        pltpu.make_async_copy(fix_in, fixed, load_sem.at[3]),
    ]
    for c in loads:
        c.start()

    if comm:
        barrier = pltpu.get_barrier_semaphore()
        near = [shifted(0, 1, 0), shifted(0, -1, 0)] + [shifted(i, j, 0) for i in (1, -1) for j in (1, -1)]
        peers = near + [by_chip(*o) for o in group_a + group_b]
        for peer in peers:
            pl.semaphore_signal(barrier, inc=1, device_id=peer, device_id_type=MESH)

    lane = lax.broadcasted_iota(jnp.int32, (8, 128), 1)
    is_last = lane == 127
    is_first = lane == 0
    is_edge = is_last | is_first
    pair = [(lane >> 1) == z for z in range(6)]
    odd16 = (lax.broadcasted_iota(jnp.int32, (16, 128), 1) & 1) == 1
    odd8 = (lane & 1) == 1
    group_of = lane >> 4
    zero = jnp.zeros((8, 128), F32)

    def gather_edges(values, g):
        packed = jnp.zeros_like(values[0])
        for z in range(6):
            packed = jnp.where(pair[z], pltpu.roll(values[z], 2 * z + 1, 1), packed)
        return pltpu.roll(packed, 16 * g, 1)

    def pack_rows(it, source):
        for c in range(2):
            for z in range(6):
                row_own[it, 0, c, z:z + 1, :] = source[c, z, 0:1, :]
                row_own[it, 1, c, z:z + 1, :] = source[c, z, 127:128, :]

    def halo_copies(it, source):
        out = []
        for side, (oz, first) in enumerate(((1, 4), (-1, 0))):
            out.append((source.at[:, pl.ds(first, 2), pl.ds(0, 128), :], z_in.at[it, side], shifted(0, 0, oz)))
        for side, (oy, which) in enumerate(((1, 1), (-1, 0))):
            out.append((row_own.at[it, which], row_in.at[it, side], shifted(0, oy, 0)))
        for slot, (ox, oy) in enumerate(COLUMN_PEERS):
            out.append((edge_own.at[it], edge_in.at[it, slot], shifted(ox, oy, 0)))
        return [
            pltpu.make_async_remote_copy(
                src_ref=s, dst_ref=d, send_sem=halo_send.at[it, n], recv_sem=halo_recv.at[it, n],
                device_id=peer, device_id_type=MESH)
            for n, (s, d, peer) in enumerate(out)
        ]

    def send_sum(it, phase, group, buffer, value):
        if not comm:
            return
        sum_src[it, phase] = value
        for k, o in enumerate(group, 1):
            pltpu.make_async_remote_copy(
                src_ref=sum_src.at[it, phase], dst_ref=buffer.at[it, k],
                send_sem=sum_send.at[it, phase], recv_sem=sum_recv.at[it, phase],
                device_id=by_chip(*o), device_id_type=MESH).start()

    def take_sum(it, phase, group, buffer, value):
        if not comm:
            return value
        got = buffer.at[it, pl.ds(1, len(group))]
        pltpu.make_async_remote_copy(
            src_ref=got, dst_ref=got, send_sem=sum_send.at[it, phase], recv_sem=sum_recv.at[it, phase],
            device_id=by_chip(*group[0]), device_id_type=MESH).wait_recv()
        for k in range(1, len(group) + 1):
            value = value + buffer[it, k]
        return value

    def wait_sums_sent(it):
        for phase, (group, buffer) in enumerate(((group_a, sum_a), (group_b, sum_b))):
            got = buffer.at[it, pl.ds(1, len(group))]
            pltpu.make_async_remote_copy(
                src_ref=got, dst_ref=got, send_sem=sum_send.at[it, phase], recv_sem=sum_recv.at[it, phase],
                device_id=by_chip(*group[0]), device_id_type=MESH).wait_send()

    row_own[...] = jnp.zeros_like(row_own)
    loads[0].wait()
    pack_rows(0, pos)

    def pack_positions(g, packed):
        out = list(packed)
        for j in range(2):
            r = pl.multiple_of(16 * g + 8 * j, 8)
            for c in range(2):
                values = [pos[c, z, pl.ds(r, 8), :] for z in range(6)]
                out[2 * c + j] = out[2 * c + j] + gather_edges(values, g)
        return tuple(out)

    packed = lax.fori_loop(0, 8, pack_positions, (zero,) * 4, unroll=4)
    for c in range(2):
        for j in range(2):
            edge_own[0, c, 8 * j:8 * j + 8, :] = packed[2 * c + j]

    if comm:
        pl.semaphore_wait(barrier, len(peers))
        copies = [halo_copies(0, pos)]
        for c in copies[0]:
            c.start()

    loads[1].wait()
    loads[3].wait()
    plane = TIME_STEP * STIFF_PLANE
    one = TIME_STEP * HUBER_DELTA * 0.5
    two = TIME_STEP * HUBER_DELTA * 0.25

    def masks(g, packed):
        out = list(packed)
        for j in range(2):
            r = pl.multiple_of(16 * g + 8 * j, 8)
            rows = pl.ds(r, 8)
            kept = []
            for z in range(6):
                code = codes[z, rows, :]
                kept.append(code)
                m_plane[0, z, rows, :] = jnp.where(is_last, 0.0, bit(code, 0, plane))
                m_plane[1, z, rows, :] = bit(code, 2, plane)
                m_plane[2, z, rows, :] = jnp.where(is_last, 0.0, bit(code, 4, plane))
                m_plane[3, z, rows, :] = jnp.where(is_last, 0.0, lanes_left(bit(code, 6, plane)))
                m_one[z + 1, rows, :] = bit(code, 8, one)
                m_two[z + 2, rows, :] = bit(code, 10, two)
                if z == 0:
                    m_one[0, rows, :] = bit(code, 9, one)
                if z < 2:
                    m_two[z, rows, :] = bit(code, 11, two)
                mov[z, rows, :] = (1 - fixed[z, rows, :]).astype(F32)
            out[j] = out[j] + gather_edges(kept, g)
        return tuple(out)

    edge_codes = lax.fori_loop(0, 8, masks, (jnp.zeros((8, 128), jnp.int32),) * 2, unroll=2)
    for j in range(2):
        for n, (first, last) in enumerate(((5, 7), (1, 0), (6, 4))):
            m_edge[n, 8 * j:8 * j + 8, :] = jnp.where(odd8, bit(edge_codes[j], first, plane), bit(edge_codes[j], last, plane))
    for z in range(6):
        code = codes[z, 0:1, :]
        line = lax.broadcasted_iota(jnp.int32, (1, 128), 1)
        m_top[0, z:z + 1, :] = bit(code, 3, plane)
        m_top[1, z:z + 1, :] = jnp.where(line == 127, 0.0, bit(code, 7, plane))
        m_top[2, z:z + 1, :] = jnp.where(line == 0, 0.0, bit(code, 5, plane))

    def build_halo(it, c):
        def got(slot, j):
            return edge_in[it, slot, c, 8 * j:8 * j + 8, :]

        near_rows = [jnp.where(odd8, lanes_right(got(FROM_LEFT, j)), lanes_left(got(FROM_RIGHT, j))) for j in range(2)]
        up = jnp.where(odd8, pltpu.roll(got(FROM_UP_LEFT, 1), 17, 1), pltpu.roll(got(FROM_UP_RIGHT, 1), 15, 1))
        down = jnp.where(odd8, pltpu.roll(got(FROM_DOWN_LEFT, 0), 113, 1), pltpu.roll(got(FROM_DOWN_RIGHT, 0), 111, 1))
        above = jnp.where(group_of == 0, up, pltpu.roll(near_rows[1], 16, 1))
        under = jnp.where(group_of == 7, down, pltpu.roll(near_rows[0], 112, 1))
        return [above, near_rows[0], near_rows[1], under]

    loads[2].wait()
    scale = None
    damp = F32(DAMPING)
    for it in range(ITERS):
        first = it == 0

        def advance(z, carry):
            for i in range(16):
                rows = slice(8 * i, 8 * i + 8)
                for c in range(2):
                    p = pos[c, z, rows, :]
                    if not first:
                        p = p + scale * kick[c, z, rows, :]
                        pos[c, z, rows, :] = p
                    p = lanes_left(p)
                    rolled[c, z, rows, :] = p + 1.0 if c else p
            return carry

        lax.fori_loop(0, 6, advance, 0, unroll=6)

        if comm:
            for n in range(2, 10):
                copies[it][n].wait_recv()

        for c in range(2):
            own, up, down = row_own[it, 0, c], row_in[it, 0, c], row_in[it, 1, c]
            edges = edge_own[it, c]
            halo = build_halo(it, c)
            if not first:
                own = row_pos[c] + scale * own
                up = up_pos[c] + scale * up
                down = down_pos[c] + scale * down
                edges = edge_pos[c] + jnp.concatenate([scale, scale], 0) * edges
                halo = [edge_halo[c, 8 * n:8 * n + 8, :] + scale * h for n, h in enumerate(halo)]
            row_pos[c], up_pos[c], down_pos[c], edge_pos[c] = own, up, down, edges
            for n, h in enumerate(halo):
                edge_halo[c, 8 * n:8 * n + 8, :] = h
            right = lanes_left(down)
            right = right + 1.0 if c else right
            for z in range(6):
                pos[c, z, 128:129, :] = down[z:z + 1, :]
                rolled[c, z, 128:129, :] = right[z:z + 1, :]

        top = [zero, zero]
        own_y, own_x, up_y, up_x = row_pos[0], row_pos[1], up_pos[0], up_pos[1]
        for n, (step, turn) in enumerate(((0, 0), (1, 127), (-1, 1))):
            ny_, nx_ = (pltpu.roll(up_y, turn, 1), pltpu.roll(up_x, turn, 1)) if turn else (up_y, up_x)
            dy, dx = ny_ - own_y - 1.0, nx_ - own_x + float(step)
            w = plane_weight(dy, dx, DIAG if step else 1.0, m_top[n])
            top = [top[0] + w * dy, top[1] + w * dx]
        for c in range(2):
            for z in range(6):
                below[c, z, 7:8, :] = -top[c][z:z + 1, :]
                below_right[c, z, 7:8, :] = jnp.zeros((1, 128), F32)

        side = [jnp.zeros((16, 128), F32)] * 2
        way = jnp.where(odd16, F32(-1.0), F32(1.0))
        own_y, own_x = edge_pos[0], edge_pos[1]
        for n, step in enumerate((-1, 0, 1)):
            dy = edge_halo[0, 8 + step:24 + step, :] - own_y + float(step)
            dx = edge_halo[1, 8 + step:24 + step, :] - own_x + way
            w = plane_weight(dy, dx, DIAG if step else 1.0, m_edge[n])
            side = [side[0] + w * dy, side[1] + w * dx]
        for c in range(2):
            edge_force[c] = side[c]

        def in_plane(z, carry):
            for i in range(16):
                r = 8 * i
                rows, next_rows = slice(r, r + 8), slice(r + 1, r + 9)
                y, x = pos[0, z, rows, :], pos[1, z, rows, :]
                y_d, x_d = pos[0, z, next_rows, :], pos[1, z, next_rows, :]
                y_r, x_r = rolled[0, z, rows, :], rolled[1, z, rows, :]
                y_dr, x_dr = rolled[0, z, next_rows, :], rolled[1, z, next_rows, :]
                y_less, y_r_less = y - 1.0, y_r - 1.0

                def link(dy, dx, rest, n):
                    w = plane_weight(dy, dx, rest, m_plane[n, z, rows, :])
                    return w * dy, w * dx

                across = link(y_r - y, x_r - x, 1.0, 0)
                down = link(y_d - y_less, x_d - x, 1.0, 1)
                diag = link(y_dr - y_less, x_dr - x, DIAG, 2)
                anti = link(y_d - y_r_less, x_d - x_r, DIAG, 3)
                for c in range(2):
                    below[c, z, r + 8:r + 16, :] = down[c] + anti[c]
                    below_right[c, z, r + 8:r + 16, :] = diag[c]
                    here = across[c] + down[c] + diag[c] - below[c, z, r + 7:r + 15, :]
                    right = anti[c] - across[c] - below_right[c, z, r + 7:r + 15, :]
                    force[c, z, rows, :] = here + lanes_right(right)
            return carry

        lax.fori_loop(0, 6, in_plane, 0)

        if comm:
            for n in range(2):
                copies[it][n].wait()

        def depth(g, carry):
            energy, packed = carry[0], list(carry[1:])
            for j in range(2):
                r = pl.multiple_of(16 * g + 8 * j, 8)
                rows = pl.ds(r, 8)
                at, got = {}, {}
                for z in range(6):
                    at[z] = [pos[c, z, rows, :] for c in range(2)]
                    got[z] = [force[c, z, rows, :] for c in range(2)]
                for s in range(2):
                    for n in range(2):
                        vals = []
                        for c in range(2):
                            v = z_in[0, s, c, n, rows, :]
                            if not first:
                                v = v + scale * z_in[it, s, c, n, rows, :]
                                if it < ITERS - 1:
                                    z_in[0, s, c, n, rows, :] = v
                            vals.append(v)
                        at[n - 2 if s == 0 else n + 6] = vals
                for reach, mask in ((1, m_one), (2, m_two)):
                    for z in range(-reach, 6):
                        a, b = at[z], at[z + reach]
                        dy, dx = b[0] - a[0], b[1] - a[1]
                        w = depth_weight(dy, dx, mask[z + reach, rows, :])
                        for c, d in enumerate((w * dy, w * dx)):
                            if z >= 0:
                                got[z][c] = got[z][c] + d
                            if z + reach < 6:
                                got[z + reach][c] = got[z + reach][c] - d
                kicked = [[], []]
                for c in range(2):
                    edge = pltpu.roll(edge_force[c, 8 * j:8 * j + 8, :], lax.rem(128 - 16 * g, 128), 1)
                    for z in range(6):
                        f = got[z][c] + jnp.where(is_edge, pltpu.roll(edge, 127 - 2 * z, 1), 0.0)
                        k = (damp * kick[c, z, rows, :] + f) * mov[z, rows, :]
                        kick[c, z, rows, :] = k
                        energy = energy + k * k
                        kicked[c].append(k)
                    if it < ITERS - 1:
                        packed[2 * c + j] = packed[2 * c + j] + gather_edges(kicked[c], g)
            return (energy, *packed)

        energy, *packed = lax.fori_loop(0, 8, depth, (zero,) * 5, unroll=4)

        if it < ITERS - 1:
            pack_rows(it + 1, kick)
            for c in range(2):
                for j in range(2):
                    edge_own[it + 1, c, 8 * j:8 * j + 8, :] = packed[2 * c + j]

        total = jnp.sum(energy, axis=0, keepdims=True)
        send_sum(it, 0, group_a, sum_a, total)
        if comm and it < ITERS - 1:
            copies.append(halo_copies(it + 1, kick))
            for c in copies[it + 1]:
                c.start()
        if it == ITERS - 1:
            outs = [
                pltpu.make_async_copy(pos.at[:, :, pl.ds(0, 128), :], pos_out, out_sem.at[0]),
                pltpu.make_async_copy(kick, kick_out, out_sem.at[1]),
            ]
            for c in outs:
                c.start()
        total = take_sum(it, 0, group_a, sum_a, total)
        send_sum(it, 1, group_b, sum_b, total)
        total = take_sum(it, 1, group_b, sum_b, total)
        kinetic = 0.5 * jnp.sum(total, axis=1, keepdims=True)
        factor = jnp.minimum(1.0, jnp.sqrt(ENERGY_CAP * nodes_all / (kinetic + EPSILON)))
        factor = jnp.broadcast_to(factor, (8, 128))
        scale = TIME_STEP * factor
        damp = DAMPING * factor

    fac_out[...] = factor
    for c in outs:
        c.wait()
    if comm:
        for it in range(ITERS):
            for c in copies[it][2:]:
                c.wait_send()
            wait_sums_sent(it)


def local(sizes, comm, positions, velocities, link_codes, fixed_nodes):
    nx, ny, nz = sizes
    _, deep, rows, cols = positions.shape
    assert (deep, rows, cols) == (6, 128, 128)
    nodes_all = deep * rows * cols * nx * ny * nz
    vmem = pltpu.VMEM
    block = (2, 6, 128, 128)
    scratch = [
        vmem((2, 6, 136, 128), F32),
        vmem((2, 6, 136, 128), F32),
        vmem(block, F32),
        vmem(block, F32),
        vmem((2, 6, 136, 128), F32),
        vmem((2, 6, 136, 128), F32),
        vmem((6, 128, 128), jnp.int32),
        vmem((6, 128, 128), jnp.int32),
        vmem((4, 6, 128, 128), F32),
        vmem((7, 128, 128), F32),
        vmem((8, 128, 128), F32),
        vmem((6, 128, 128), F32),
        vmem((ITERS, 2, 2, 2, 128, 128), F32),
        vmem((ITERS, 2, 16, 128), F32),
        vmem((ITERS, 6, 2, 16, 128), F32),
        vmem((ITERS, 2, 2, 8, 128), F32),
        vmem((ITERS, 2, 2, 8, 128), F32),
        vmem((2, 16, 128), F32),
        vmem((2, 32, 128), F32),
        vmem((2, 8, 128), F32),
        vmem((2, 8, 128), F32),
        vmem((2, 8, 128), F32),
        vmem((3, 16, 128), F32),
        vmem((3, 8, 128), F32),
        vmem((2, 16, 128), F32),
        vmem((ITERS, 2, 1, 128), F32),
        vmem((ITERS, 2 * nx, 1, 128), F32),
        vmem((ITERS, ny // 2 * nz, 1, 128), F32),
        pltpu.SemaphoreType.DMA((4,)),
        pltpu.SemaphoreType.DMA((2,)),
        pltpu.SemaphoreType.DMA((ITERS, 10)),
        pltpu.SemaphoreType.DMA((ITERS, 10)),
        pltpu.SemaphoreType.DMA((ITERS, 2)),
        pltpu.SemaphoreType.DMA((ITERS, 2)),
    ]
    anywhere = pl.BlockSpec(memory_space=pltpu.MemorySpace.HBM)
    position, kicked, factor = pl.pallas_call(
        functools.partial(kernel, (nx, ny, nz, nodes_all), comm),
        out_shape=(
            jax.ShapeDtypeStruct(block, F32),
            jax.ShapeDtypeStruct(block, F32),
            jax.ShapeDtypeStruct((8, 128), F32),
        ),
        in_specs=[anywhere] * 4,
        out_specs=(anywhere, anywhere, pl.BlockSpec(memory_space=pltpu.VMEM)),
        scratch_shapes=scratch,
        compiler_params=pltpu.CompilerParams(
            collective_id=0 if comm else None, has_side_effects=True, vmem_limit_bytes=60 * 1024 * 1024),
    )(positions, velocities, link_codes, fixed_nodes)
    tiles = (2, deep, rows // 8, 8, cols)
    velocity = factor * kicked.reshape(tiles)
    position = position.reshape(tiles) + TIME_STEP * velocity
    return (position.reshape(block), velocity.reshape(block))


def solution(mesh, comm=True):
    sizes = tuple(mesh.shape[a] for a in AXES)
    in_specs = (
        P(None, "gz", "gy", "gx"),
        P(None, "gz", "gy", "gx"),
        P("gz", "gy", "gx"),
        P("gz", "gy", "gx"),
    )
    out_specs = (P(None, "gz", "gy", "gx"), P(None, "gz", "gy", "gx"))
    return jax.shard_map(
        functools.partial(local, sizes, comm), mesh=mesh, in_specs=in_specs, out_specs=out_specs, check_vma=False)
```

```python
import functools
import itertools
import math

import jax
import jax.numpy as jnp
from jax import lax
from jax.experimental import pallas as pl
from jax.experimental.pallas import tpu as pltpu
from jax.sharding import PartitionSpec as P

MESH = pl.DeviceIdType.MESH
ITERS = 3
TIME_STEP = 0.3
DAMPING = 0.9
STIFF_PLANE = 1.0
HUBER_DELTA = 0.5
LENGTH_FLOOR = 0.25
ENERGY_CAP = 0.04
EPSILON = 1e-06
DIAG = math.sqrt(2.0)
AXES = ("gx", "gy", "gz")
F32 = jnp.float32

COLUMN_PEERS = ((1, 0), (-1, 0), (1, 1), (-1, 1), (1, -1), (-1, -1))
FROM_LEFT, FROM_RIGHT, FROM_UP_LEFT, FROM_UP_RIGHT, FROM_DOWN_LEFT, FROM_DOWN_RIGHT = range(6)


def lanes_left(a):
    return pltpu.roll(a, 127, 1)


def lanes_right(a):
    return pltpu.roll(a, 1, 1)


def plane_weight(dy, dx, rest, mask):
    square = dy * dy + dx * dx
    u = jnp.minimum(lax.rsqrt(square), 1.0 / LENGTH_FLOOR)
    stretch = jnp.clip(square * u - rest, -HUBER_DELTA, HUBER_DELTA)
    return stretch * u * mask


def depth_weight(dy, dx, mask):
    square = dy * dy + dx * dx
    return jnp.minimum(lax.rsqrt(square), 1.0 / HUBER_DELTA) * mask


def bit(codes, index, scale):
    return jnp.where((codes & (1 << index)) != 0, F32(scale), F32(0.0))


def kernel(sizes, comm, *refs):
    (pos_in, vel_in, code_in, fix_in, pos_out, kick_out, fac_out,
     pos, rolled, kick, force, below, below_right, codes, fixed, m_plane, m_one, m_two, mov,
     z_in, edge_own, edge_in, row_own, row_in, edge_pos, edge_halo, row_pos, up_pos, down_pos,
     m_edge, m_top, edge_force, sum_src, sum_a, sum_b,
     load_sem, out_sem, halo_send, halo_recv, sum_send, sum_recv, greeted) = refs
    nx, ny, nz, nodes_all = sizes
    chips = ny // 2
    me = {a: lax.axis_index(a) for a in AXES}

    def shifted(ox, oy, oz):
        return (lax.rem(me["gx"] + ox + nx, nx), lax.rem(me["gy"] + oy + ny, ny), lax.rem(me["gz"] + oz + nz, nz))

    def by_chip(ox, chip, core, oz):
        gy = me["gy"]
        where = lax.rem(lax.div(gy, 2) + chip, chips) * 2 + lax.rem(lax.rem(gy, 2) + core, 2)
        return (lax.rem(me["gx"] + ox, nx), where, lax.rem(me["gz"] + oz, nz))

    def far(o):
        ox, chip, core, oz = o
        return -(min(ox, nx - ox) + min(chip, chips - chip) + min(oz, nz - oz)) - 0.1 * core

    group_a = sorted([(i, 0, c, 0) for i in range(nx) for c in range(2) if i or c], key=far)
    group_b = sorted([(0, c, 0, k) for c in range(chips) for k in range(nz) if c or k], key=far)

    loads = [
        pltpu.make_async_copy(pos_in, pos.at[:, :, pl.ds(0, 128), :], load_sem.at[0]),
        pltpu.make_async_copy(code_in, codes, load_sem.at[1]),
        pltpu.make_async_copy(vel_in, kick, load_sem.at[2]),
        pltpu.make_async_copy(fix_in, fixed, load_sem.at[3]),
    ]
    for c in loads:
        c.start()

    if comm:
        barrier = pltpu.get_barrier_semaphore()
        beside = [(1, 0, 0, 0), (nx - 1, 0, 0, 0), (0, 0, 0, 1), (0, 0, 0, nz - 1),
                  (0, 1, 0, 0), (0, chips - 1, 0, 0), (0, 0, 1, 0)]
        peers = [shifted(i, j, 0) for i in (1, -1, 0) for j in (1, -1)] + [by_chip(*o) for o in beside]
        for peer in peers:
            pl.semaphore_signal(barrier, inc=1, device_id=peer, device_id_type=MESH)
    rounds = [
        [(1, 0, 0, 0), (nx - 1, 0, 0, 0), (0, 0, 0, 1), (0, 0, 0, nz - 1), (0, 1, 0, 0), (0, chips - 1, 0, 0), (0, 0, 1, 0)],
        [(2 % nx, 0, 0, 0), (nx - 2, 0, 0, 0), (0, 0, 0, 2 % nz), (0, 0, 0, nz - 2)],
        [(0, 0, 1, 0), (0, 1, 0, 0), (0, 2 % chips, 0, 0), (0, chips - 1, 0, 0)],
    ]

    def greet(n):
        if comm:
            for o in rounds[n]:
                pl.semaphore_signal(greeted.at[n], inc=1, device_id=by_chip(*o), device_id_type=MESH)

    def meet(n):
        if comm:
            pl.semaphore_wait(greeted.at[n], len(rounds[n]))

    lane = lax.broadcasted_iota(jnp.int32, (8, 128), 1)
    is_last = lane == 127
    is_first = lane == 0
    is_edge = is_last | is_first
    pair = [(lane >> 1) == z for z in range(6)]
    odd16 = (lax.broadcasted_iota(jnp.int32, (16, 128), 1) & 1) == 1
    odd8 = (lane & 1) == 1
    group_of = lane >> 4
    zero = jnp.zeros((8, 128), F32)

    def gather_edges(values, g):
        packed = jnp.zeros_like(values[0])
        for z in range(6):
            packed = jnp.where(pair[z], pltpu.roll(values[z], 2 * z + 1, 1), packed)
        return pltpu.roll(packed, 16 * g, 1)

    def pack_rows(it, source):
        for c in range(2):
            for z in range(6):
                row_own[it, 0, c, z:z + 1, :] = source[c, z, 0:1, :]
                row_own[it, 1, c, z:z + 1, :] = source[c, z, 127:128, :]

    def halo_copies(it, source):
        out = []
        for side, (oz, first) in enumerate(((1, 4), (-1, 0))):
            out.append((source.at[:, pl.ds(first, 2), pl.ds(0, 128), :], z_in.at[it, side], shifted(0, 0, oz)))
        for side, (oy, which) in enumerate(((1, 1), (-1, 0))):
            out.append((row_own.at[it, which], row_in.at[it, side], shifted(0, oy, 0)))
        for slot, (ox, oy) in enumerate(COLUMN_PEERS):
            out.append((edge_own.at[it], edge_in.at[it, slot], shifted(ox, oy, 0)))
        return [
            pltpu.make_async_remote_copy(
                src_ref=s, dst_ref=d, send_sem=halo_send.at[it, n], recv_sem=halo_recv.at[it, n],
                device_id=peer, device_id_type=MESH)
            for n, (s, d, peer) in enumerate(out)
        ]

    def send_sum(it, phase, group, buffer, value):
        if not comm:
            return
        sum_src[it, phase] = value
        for k, o in enumerate(group, 1):
            pltpu.make_async_remote_copy(
                src_ref=sum_src.at[it, phase], dst_ref=buffer.at[it, k],
                send_sem=sum_send.at[it, phase], recv_sem=sum_recv.at[it, phase],
                device_id=by_chip(*o), device_id_type=MESH).start()

    def take_sum(it, phase, group, buffer, value):
        if not comm:
            return value
        got = buffer.at[it, pl.ds(1, len(group))]
        pltpu.make_async_remote_copy(
            src_ref=got, dst_ref=got, send_sem=sum_send.at[it, phase], recv_sem=sum_recv.at[it, phase],
            device_id=by_chip(*group[0]), device_id_type=MESH).wait_recv()
        terms = [value] + [buffer[it, k] for k in range(1, len(group) + 1)]
        while len(terms) > 1:
            terms = [a + b for a, b in zip(terms[::2], terms[1::2])] + (terms[-1:] if len(terms) % 2 else [])
        return terms[0]

    def wait_sums_sent(it):
        for phase, (group, buffer) in enumerate(((group_a, sum_a), (group_b, sum_b))):
            got = buffer.at[it, pl.ds(1, len(group))]
            pltpu.make_async_remote_copy(
                src_ref=got, dst_ref=got, send_sem=sum_send.at[it, phase], recv_sem=sum_recv.at[it, phase],
                device_id=by_chip(*group[0]), device_id_type=MESH).wait_send()

    row_own[...] = jnp.zeros_like(row_own)
    loads[0].wait()
    if comm:
        pl.semaphore_wait(barrier, len(peers))
        copies = [halo_copies(0, pos)]
        for c in copies[0][:2]:
            c.start()
    greet(0)
    pack_rows(0, pos)

    def pack_positions(g, packed):
        out = list(packed)
        for j in range(2):
            r = pl.multiple_of(16 * g + 8 * j, 8)
            for c in range(2):
                values = [pos[c, z, pl.ds(r, 8), :] for z in range(6)]
                out[2 * c + j] = out[2 * c + j] + gather_edges(values, g)
        return tuple(out)

    packed = lax.fori_loop(0, 8, pack_positions, (zero,) * 4, unroll=4)
    for c in range(2):
        for j in range(2):
            edge_own[0, c, 8 * j:8 * j + 8, :] = packed[2 * c + j]

    if comm:
        for c in copies[0][2:]:
            c.start()
    meet(0)
    greet(1)

    loads[1].wait()
    loads[3].wait()
    plane = TIME_STEP * STIFF_PLANE
    one = TIME_STEP * HUBER_DELTA * 0.5
    two = TIME_STEP * HUBER_DELTA * 0.25

    def masks(g, packed):
        out = list(packed)
        for j in range(2):
            r = pl.multiple_of(16 * g + 8 * j, 8)
            rows = pl.ds(r, 8)
            kept = []
            for z in range(6):
                code = codes[z, rows, :]
                kept.append(code)
                m_plane[0, z, rows, :] = jnp.where(is_last, 0.0, bit(code, 0, plane))
                m_plane[1, z, rows, :] = bit(code, 2, plane)
                m_plane[2, z, rows, :] = jnp.where(is_last, 0.0, bit(code, 4, plane))
                m_plane[3, z, rows, :] = jnp.where(is_last, 0.0, lanes_left(bit(code, 6, plane)))
                m_one[z + 1, rows, :] = bit(code, 8, one)
                m_two[z + 2, rows, :] = bit(code, 10, two)
                if z == 0:
                    m_one[0, rows, :] = bit(code, 9, one)
                if z < 2:
                    m_two[z, rows, :] = bit(code, 11, two)
                mov[z, rows, :] = (1 - fixed[z, rows, :]).astype(F32)
            out[j] = out[j] + gather_edges(kept, g)
        return tuple(out)

    edge_codes = lax.fori_loop(0, 8, masks, (jnp.zeros((8, 128), jnp.int32),) * 2, unroll=2)
    for j in range(2):
        for n, (first, last) in enumerate(((5, 7), (1, 0), (6, 4))):
            m_edge[n, 8 * j:8 * j + 8, :] = jnp.where(odd8, bit(edge_codes[j], first, plane), bit(edge_codes[j], last, plane))
    for z in range(6):
        code = codes[z, 0:1, :]
        line = lax.broadcasted_iota(jnp.int32, (1, 128), 1)
        m_top[0, z:z + 1, :] = bit(code, 3, plane)
        m_top[1, z:z + 1, :] = jnp.where(line == 127, 0.0, bit(code, 7, plane))
        m_top[2, z:z + 1, :] = jnp.where(line == 0, 0.0, bit(code, 5, plane))

    def build_halo(it, c):
        def got(slot, j):
            return edge_in[it, slot, c, 8 * j:8 * j + 8, :]

        near_rows = [jnp.where(odd8, lanes_right(got(FROM_LEFT, j)), lanes_left(got(FROM_RIGHT, j))) for j in range(2)]
        up = jnp.where(odd8, pltpu.roll(got(FROM_UP_LEFT, 1), 17, 1), pltpu.roll(got(FROM_UP_RIGHT, 1), 15, 1))
        down = jnp.where(odd8, pltpu.roll(got(FROM_DOWN_LEFT, 0), 113, 1), pltpu.roll(got(FROM_DOWN_RIGHT, 0), 111, 1))
        above = jnp.where(group_of == 0, up, pltpu.roll(near_rows[1], 16, 1))
        under = jnp.where(group_of == 7, down, pltpu.roll(near_rows[0], 112, 1))
        return [above, near_rows[0], near_rows[1], under]

    loads[2].wait()
    scale = None
    damp = F32(DAMPING)
    for it in range(ITERS):
        first = it == 0

        def advance(z, carry):
            for i in range(16):
                rows = slice(8 * i, 8 * i + 8)
                for c in range(2):
                    p = pos[c, z, rows, :]
                    if not first:
                        p = p + scale * kick[c, z, rows, :]
                        pos[c, z, rows, :] = p
                    p = lanes_left(p)
                    rolled[c, z, rows, :] = p + 1.0 if c else p
            return carry

        lax.fori_loop(0, 6, advance, 0, unroll=6)

        if first:
            meet(1)
            greet(2)
        if comm:
            for n in range(2, 10):
                copies[it][n].wait_recv()

        for c in range(2):
            own, up, down = row_own[it, 0, c], row_in[it, 0, c], row_in[it, 1, c]
            edges = edge_own[it, c]
            halo = build_halo(it, c)
            if not first:
                own = row_pos[c] + scale * own
                up = up_pos[c] + scale * up
                down = down_pos[c] + scale * down
                edges = edge_pos[c] + jnp.concatenate([scale, scale], 0) * edges
                halo = [edge_halo[c, 8 * n:8 * n + 8, :] + scale * h for n, h in enumerate(halo)]
            row_pos[c], up_pos[c], down_pos[c], edge_pos[c] = own, up, down, edges
            for n, h in enumerate(halo):
                edge_halo[c, 8 * n:8 * n + 8, :] = h
            right = lanes_left(down)
            right = right + 1.0 if c else right
            for z in range(6):
                pos[c, z, 128:129, :] = down[z:z + 1, :]
                rolled[c, z, 128:129, :] = right[z:z + 1, :]

        top = [zero, zero]
        own_y, own_x, up_y, up_x = row_pos[0], row_pos[1], up_pos[0], up_pos[1]
        for n, (step, turn) in enumerate(((0, 0), (1, 127), (-1, 1))):
            ny_, nx_ = (pltpu.roll(up_y, turn, 1), pltpu.roll(up_x, turn, 1)) if turn else (up_y, up_x)
            dy, dx = ny_ - own_y - 1.0, nx_ - own_x + float(step)
            w = plane_weight(dy, dx, DIAG if step else 1.0, m_top[n])
            top = [top[0] + w * dy, top[1] + w * dx]
        for c in range(2):
            for z in range(6):
                below[c, z, 7:8, :] = -top[c][z:z + 1, :]
                below_right[c, z, 7:8, :] = jnp.zeros((1, 128), F32)

        side = [jnp.zeros((16, 128), F32)] * 2
        way = jnp.where(odd16, F32(-1.0), F32(1.0))
        own_y, own_x = edge_pos[0], edge_pos[1]
        for n, step in enumerate((-1, 0, 1)):
            dy = edge_halo[0, 8 + step:24 + step, :] - own_y + float(step)
            dx = edge_halo[1, 8 + step:24 + step, :] - own_x + way
            w = plane_weight(dy, dx, DIAG if step else 1.0, m_edge[n])
            side = [side[0] + w * dy, side[1] + w * dx]
        for c in range(2):
            edge_force[c] = side[c]

        def in_plane(z, carry):
            for i in range(16):
                r = 8 * i
                rows, next_rows = slice(r, r + 8), slice(r + 1, r + 9)
                y, x = pos[0, z, rows, :], pos[1, z, rows, :]
                y_d, x_d = pos[0, z, next_rows, :], pos[1, z, next_rows, :]
                y_r, x_r = rolled[0, z, rows, :], rolled[1, z, rows, :]
                y_dr, x_dr = rolled[0, z, next_rows, :], rolled[1, z, next_rows, :]
                y_less, y_r_less = y - 1.0, y_r - 1.0

                def link(dy, dx, rest, n):
                    w = plane_weight(dy, dx, rest, m_plane[n, z, rows, :])
                    return w * dy, w * dx

                across = link(y_r - y, x_r - x, 1.0, 0)
                down = link(y_d - y_less, x_d - x, 1.0, 1)
                diag = link(y_dr - y_less, x_dr - x, DIAG, 2)
                anti = link(y_d - y_r_less, x_d - x_r, DIAG, 3)
                for c in range(2):
                    below[c, z, r + 8:r + 16, :] = down[c] + anti[c]
                    below_right[c, z, r + 8:r + 16, :] = diag[c]
                    here = across[c] + down[c] + diag[c] - below[c, z, r + 7:r + 15, :]
                    right = anti[c] - across[c] - below_right[c, z, r + 7:r + 15, :]
                    force[c, z, rows, :] = here + lanes_right(right)
            return carry

        lax.fori_loop(0, 6, in_plane, 0)

        if first:
            meet(2)
        if comm:
            for n in range(2):
                copies[it][n].wait()

        def depth(g, carry):
            energy, packed = carry[0], list(carry[1:])
            for j in range(2):
                r = pl.multiple_of(16 * g + 8 * j, 8)
                rows = pl.ds(r, 8)
                at, got = {}, {}
                for z in range(6):
                    at[z] = [pos[c, z, rows, :] for c in range(2)]
                    got[z] = [force[c, z, rows, :] for c in range(2)]
                for s in range(2):
                    for n in range(2):
                        vals = []
                        for c in range(2):
                            v = z_in[0, s, c, n, rows, :]
                            if not first:
                                v = v + scale * z_in[it, s, c, n, rows, :]
                                if it < ITERS - 1:
                                    z_in[0, s, c, n, rows, :] = v
                            vals.append(v)
                        at[n - 2 if s == 0 else n + 6] = vals
                for reach, mask in ((1, m_one), (2, m_two)):
                    for z in range(-reach, 6):
                        a, b = at[z], at[z + reach]
                        dy, dx = b[0] - a[0], b[1] - a[1]
                        w = depth_weight(dy, dx, mask[z + reach, rows, :])
                        for c, d in enumerate((w * dy, w * dx)):
                            if z >= 0:
                                got[z][c] = got[z][c] + d
                            if z + reach < 6:
                                got[z + reach][c] = got[z + reach][c] - d
                kicked = [[], []]
                for c in range(2):
                    edge = pltpu.roll(edge_force[c, 8 * j:8 * j + 8, :], lax.rem(128 - 16 * g, 128), 1)
                    for z in range(6):
                        f = got[z][c] + jnp.where(is_edge, pltpu.roll(edge, 127 - 2 * z, 1), 0.0)
                        k = (damp * kick[c, z, rows, :] + f) * mov[z, rows, :]
                        kick[c, z, rows, :] = k
                        energy = energy + k * k
                        kicked[c].append(k)
                    if it < ITERS - 1:
                        packed[2 * c + j] = packed[2 * c + j] + gather_edges(kicked[c], g)
            return (energy, *packed)

        energy, *packed = lax.fori_loop(0, 8, depth, (zero,) * 5, unroll=4)

        if it < ITERS - 1:
            pack_rows(it + 1, kick)
            for c in range(2):
                for j in range(2):
                    edge_own[it + 1, c, 8 * j:8 * j + 8, :] = packed[2 * c + j]

        total = jnp.sum(energy, axis=0, keepdims=True)
        send_sum(it, 0, group_a, sum_a, total)
        if comm and it < ITERS - 1:
            copies.append(halo_copies(it + 1, kick))
            for c in copies[it + 1]:
                c.start()
        if it == ITERS - 1:
            outs = [
                pltpu.make_async_copy(pos.at[:, :, pl.ds(0, 128), :], pos_out, out_sem.at[0]),
                pltpu.make_async_copy(kick, kick_out, out_sem.at[1]),
            ]
            for c in outs:
                c.start()
        total = take_sum(it, 0, group_a, sum_a, total)
        send_sum(it, 1, group_b, sum_b, total)
        total = take_sum(it, 1, group_b, sum_b, total)
        kinetic = 0.5 * jnp.sum(total, axis=1, keepdims=True)
        factor = jnp.minimum(1.0, jnp.sqrt(ENERGY_CAP * nodes_all / (kinetic + EPSILON)))
        factor = jnp.broadcast_to(factor, (8, 128))
        scale = TIME_STEP * factor
        damp = DAMPING * factor

    fac_out[...] = factor
    for c in outs:
        c.wait()
    if comm:
        for it in range(ITERS):
            for c in copies[it][2:]:
                c.wait_send()
            wait_sums_sent(it)


def local(sizes, comm, positions, velocities, link_codes, fixed_nodes):
    nx, ny, nz = sizes
    _, deep, rows, cols = positions.shape
    assert (deep, rows, cols) == (6, 128, 128)
    nodes_all = deep * rows * cols * nx * ny * nz
    vmem = pltpu.VMEM
    block = (2, 6, 128, 128)
    scratch = [
        vmem((2, 6, 136, 128), F32),
        vmem((2, 6, 136, 128), F32),
        vmem(block, F32),
        vmem(block, F32),
        vmem((2, 6, 136, 128), F32),
        vmem((2, 6, 136, 128), F32),
        vmem((6, 128, 128), jnp.int32),
        vmem((6, 128, 128), jnp.int32),
        vmem((4, 6, 128, 128), F32),
        vmem((7, 128, 128), F32),
        vmem((8, 128, 128), F32),
        vmem((6, 128, 128), F32),
        vmem((ITERS, 2, 2, 2, 128, 128), F32),
        vmem((ITERS, 2, 16, 128), F32),
        vmem((ITERS, 6, 2, 16, 128), F32),
        vmem((ITERS, 2, 2, 8, 128), F32),
        vmem((ITERS, 2, 2, 8, 128), F32),
        vmem((2, 16, 128), F32),
        vmem((2, 32, 128), F32),
        vmem((2, 8, 128), F32),
        vmem((2, 8, 128), F32),
        vmem((2, 8, 128), F32),
        vmem((3, 16, 128), F32),
        vmem((3, 8, 128), F32),
        vmem((2, 16, 128), F32),
        vmem((ITERS, 2, 1, 128), F32),
        vmem((ITERS, 2 * nx, 1, 128), F32),
        vmem((ITERS, ny // 2 * nz, 1, 128), F32),
        pltpu.SemaphoreType.DMA((4,)),
        pltpu.SemaphoreType.DMA((2,)),
        pltpu.SemaphoreType.DMA((ITERS, 10)),
        pltpu.SemaphoreType.DMA((ITERS, 10)),
        pltpu.SemaphoreType.DMA((ITERS, 2)),
        pltpu.SemaphoreType.DMA((ITERS, 2)),
        pltpu.SemaphoreType.REGULAR((3,)),
    ]
    anywhere = pl.BlockSpec(memory_space=pltpu.MemorySpace.HBM)
    position, kicked, factor = pl.pallas_call(
        functools.partial(kernel, (nx, ny, nz, nodes_all), comm),
        out_shape=(
            pltpu.VMEM(block, F32),
            pltpu.VMEM(block, F32),
            pltpu.VMEM((8, 128), F32),
        ),
        in_specs=[anywhere] * 4,
        out_specs=(pl.BlockSpec(memory_space=pltpu.VMEM),) * 3,
        scratch_shapes=scratch,
        compiler_params=pltpu.CompilerParams(
            collective_id=0 if comm else None, has_side_effects=True, vmem_limit_bytes=32 * 1024 * 1024),
    )(*(pltpu.with_memory_space_constraint(a, pltpu.HBM) for a in (positions, velocities, link_codes, fixed_nodes)))
    tiles = (2, deep, rows // 8, 8, cols)
    velocity = factor * kicked.reshape(tiles)
    position = position.reshape(tiles) + TIME_STEP * velocity
    return (position.reshape(block), velocity.reshape(block))


def solution(mesh, comm=True):
    sizes = tuple(mesh.shape[a] for a in AXES)
    in_specs = (
        P(None, "gz", "gy", "gx"),
        P(None, "gz", "gy", "gx"),
        P("gz", "gy", "gx"),
        P("gz", "gy", "gx"),
    )
    out_specs = (P(None, "gz", "gy", "gx"), P(None, "gz", "gy", "gx"))
    return jax.shard_map(
        functools.partial(local, sizes, comm), mesh=mesh, in_specs=in_specs, out_specs=out_specs, check_vma=False)
```

```python
import functools
import itertools
import math

import jax
import jax.numpy as jnp
from jax import lax
from jax.experimental import pallas as pl
from jax.experimental.pallas import tpu as pltpu
from jax.sharding import PartitionSpec as P

MESH = pl.DeviceIdType.MESH
ITERS = 3
TIME_STEP = 0.3
DAMPING = 0.9
STIFF_PLANE = 1.0
HUBER_DELTA = 0.5
LENGTH_FLOOR = 0.25
ENERGY_CAP = 0.04
EPSILON = 1e-06
DIAG = math.sqrt(2.0)
AXES = ("gx", "gy", "gz")
F32 = jnp.float32

COLUMN_PEERS = ((1, 0), (-1, 0), (1, 1), (-1, 1), (1, -1), (-1, -1))
FROM_LEFT, FROM_RIGHT, FROM_UP_LEFT, FROM_UP_RIGHT, FROM_DOWN_LEFT, FROM_DOWN_RIGHT = range(6)


def lanes_left(a):
    return pltpu.roll(a, 127, 1)


def lanes_right(a):
    return pltpu.roll(a, 1, 1)


def plane_weight(dy, dx, rest, mask):
    square = dy * dy + dx * dx
    u = jnp.minimum(lax.rsqrt(square), 1.0 / LENGTH_FLOOR)
    stretch = jnp.clip(square * u - rest, -HUBER_DELTA, HUBER_DELTA)
    return stretch * u * mask


def depth_weight(dy, dx, mask):
    square = dy * dy + dx * dx
    return jnp.minimum(lax.rsqrt(square), 1.0 / HUBER_DELTA) * mask


def bit(codes, index, scale):
    return jnp.where((codes & (1 << index)) != 0, F32(scale), F32(0.0))


def kernel(sizes, comm, *refs):
    (pos_in, vel_in, code_in, fix_in, pos_out, kick_out, fac_out,
     pos, rolled, kick, force, below, below_right, codes, fixed, m_plane, m_one, m_two, mov,
     z_in, edge_own, edge_in, row_own, row_in, edge_pos, edge_halo, row_pos, up_pos, down_pos,
     m_edge, m_top, edge_force, edge_next, sum_src, sum_a, sum_b,
     load_sem, out_sem, halo_send, halo_recv, sum_send, sum_recv, greeted) = refs
    nx, ny, nz, nodes_all = sizes
    chips = ny // 2
    me = {a: lax.axis_index(a) for a in AXES}

    def shifted(ox, oy, oz):
        return (lax.rem(me["gx"] + ox + nx, nx), lax.rem(me["gy"] + oy + ny, ny), lax.rem(me["gz"] + oz + nz, nz))

    def by_chip(ox, chip, core, oz):
        gy = me["gy"]
        where = lax.rem(lax.div(gy, 2) + chip, chips) * 2 + lax.rem(lax.rem(gy, 2) + core, 2)
        return (lax.rem(me["gx"] + ox, nx), where, lax.rem(me["gz"] + oz, nz))

    def far(o):
        ox, chip, core, oz = o
        return -(min(ox, nx - ox) + min(chip, chips - chip) + min(oz, nz - oz)) - 0.1 * core

    group_a = sorted([(0, c, k, 0) for c in range(chips) for k in range(2) if c or k], key=far)
    group_b = sorted([(i, 0, 0, k) for i in range(nx) for k in range(nz) if i or k], key=far)

    loads = [
        pltpu.make_async_copy(pos_in, pos.at[:, :, pl.ds(0, 128), :], load_sem.at[0]),
        pltpu.make_async_copy(code_in, codes, load_sem.at[1]),
        pltpu.make_async_copy(vel_in, kick, load_sem.at[2]),
        pltpu.make_async_copy(fix_in, fixed, load_sem.at[3]),
    ]
    for c in loads:
        c.start()

    if comm:
        barrier = pltpu.get_barrier_semaphore()
        beside = [(1, 0, 0, 0), (nx - 1, 0, 0, 0), (0, 0, 0, 1), (0, 0, 0, nz - 1),
                  (0, 1, 0, 0), (0, chips - 1, 0, 0), (0, 0, 1, 0)]
        peers = [shifted(i, j, 0) for i in (1, -1, 0) for j in (1, -1)] + [by_chip(*o) for o in beside]
        for peer in peers:
            pl.semaphore_signal(barrier, inc=1, device_id=peer, device_id_type=MESH)
    rounds = [
        [(1, 0, 0, 0), (nx - 1, 0, 0, 0), (0, 0, 0, 1), (0, 0, 0, nz - 1), (0, 1, 0, 0), (0, chips - 1, 0, 0), (0, 0, 1, 0)],
        [(2, 0, 0, 0), (nx - 2, 0, 0, 0), (0, 0, 0, 2), (0, 0, 0, nz - 2), (0, 0, 1, 0)],
        [(0, 0, 0, k) for k in range(1, nz)],
    ]

    def greet(n):
        if comm:
            for o in rounds[n]:
                pl.semaphore_signal(greeted.at[n], inc=1, device_id=by_chip(*o), device_id_type=MESH)

    def meet(n):
        if comm:
            pl.semaphore_wait(greeted.at[n], len(rounds[n]))

    lane = lax.broadcasted_iota(jnp.int32, (8, 128), 1)
    is_last = lane == 127
    is_first = lane == 0
    is_edge = is_last | is_first
    pair = [(lane >> 1) == z for z in range(6)]
    odd16 = (lax.broadcasted_iota(jnp.int32, (16, 128), 1) & 1) == 1
    odd8 = (lane & 1) == 1
    group_of = lane >> 4
    zero = jnp.zeros((8, 128), F32)

    def gather_edges(values, g):
        packed = jnp.zeros_like(values[0])
        for z in range(6):
            packed = jnp.where(pair[z], pltpu.roll(values[z], 2 * z + 1, 1), packed)
        return pltpu.roll(packed, 16 * g, 1)

    def pack_rows(it, source):
        for c in range(2):
            for z in range(6):
                row_own[it, 0, c, z:z + 1, :] = source[c, z, 0:1, :]
                row_own[it, 1, c, z:z + 1, :] = source[c, z, 127:128, :]

    def halo_copies(it, source):
        out = []
        for side, (oz, first) in enumerate(((1, 4), (-1, 0))):
            out.append((source.at[:, pl.ds(first, 2), pl.ds(0, 128), :], z_in.at[it, side], shifted(0, 0, oz)))
        for side, (oy, which) in enumerate(((1, 1), (-1, 0))):
            out.append((row_own.at[it, which], row_in.at[it, side], shifted(0, oy, 0)))
        for slot, (ox, oy) in enumerate(COLUMN_PEERS):
            out.append((edge_own.at[it], edge_in.at[it, slot], shifted(ox, oy, 0)))
        return [
            pltpu.make_async_remote_copy(
                src_ref=s, dst_ref=d, send_sem=halo_send.at[it, n], recv_sem=halo_recv.at[it, n],
                device_id=peer, device_id_type=MESH)
            for n, (s, d, peer) in enumerate(out)
        ]

    def send_sum(it, phase, group, buffer, value):
        if not comm:
            return
        sum_src[it, phase] = value
        for k, o in enumerate(group, 1):
            pltpu.make_async_remote_copy(
                src_ref=sum_src.at[it, phase], dst_ref=buffer.at[it, k],
                send_sem=sum_send.at[it, phase], recv_sem=sum_recv.at[it, phase],
                device_id=by_chip(*o), device_id_type=MESH).start()

    def take_sum(it, phase, group, buffer, value):
        if not comm:
            return value
        got = buffer.at[it, pl.ds(1, len(group))]
        pltpu.make_async_remote_copy(
            src_ref=got, dst_ref=got, send_sem=sum_send.at[it, phase], recv_sem=sum_recv.at[it, phase],
            device_id=by_chip(*group[0]), device_id_type=MESH).wait_recv()
        terms = [value] + [buffer[it, k] for k in range(1, len(group) + 1)]
        while len(terms) > 1:
            terms = [a + b for a, b in zip(terms[::2], terms[1::2])] + (terms[-1:] if len(terms) % 2 else [])
        return terms[0]

    def wait_sums_sent(it):
        for phase, (group, buffer) in enumerate(((group_a, sum_a), (group_b, sum_b))):
            got = buffer.at[it, pl.ds(1, len(group))]
            pltpu.make_async_remote_copy(
                src_ref=got, dst_ref=got, send_sem=sum_send.at[it, phase], recv_sem=sum_recv.at[it, phase],
                device_id=by_chip(*group[0]), device_id_type=MESH).wait_send()

    row_own[...] = jnp.zeros_like(row_own)
    loads[0].wait()
    if comm:
        pl.semaphore_wait(barrier, len(peers))
        copies = [halo_copies(0, pos)]
        for c in copies[0][:2]:
            c.start()
    greet(0)
    pack_rows(0, pos)

    def pack_positions(g, packed):
        out = list(packed)
        for j in range(2):
            r = pl.multiple_of(16 * g + 8 * j, 8)
            for c in range(2):
                values = [pos[c, z, pl.ds(r, 8), :] for z in range(6)]
                out[2 * c + j] = out[2 * c + j] + gather_edges(values, g)
        return tuple(out)

    packed = lax.fori_loop(0, 8, pack_positions, (zero,) * 4, unroll=4)
    for c in range(2):
        for j in range(2):
            edge_own[0, c, 8 * j:8 * j + 8, :] = packed[2 * c + j]

    if comm:
        for c in copies[0][2:]:
            c.start()
    meet(0)
    greet(1)

    loads[1].wait()
    loads[3].wait()
    plane = TIME_STEP * STIFF_PLANE
    one = TIME_STEP * HUBER_DELTA * 0.5
    two = TIME_STEP * HUBER_DELTA * 0.25

    def masks(g, packed):
        out = list(packed)
        for j in range(2):
            r = pl.multiple_of(16 * g + 8 * j, 8)
            rows = pl.ds(r, 8)
            kept = []
            for z in range(6):
                code = codes[z, rows, :]
                kept.append(code)
                m_plane[0, z, rows, :] = jnp.where(is_last, 0.0, bit(code, 0, plane))
                m_plane[1, z, rows, :] = bit(code, 2, plane)
                m_plane[2, z, rows, :] = jnp.where(is_last, 0.0, bit(code, 4, plane))
                m_plane[3, z, rows, :] = jnp.where(is_last, 0.0, lanes_left(bit(code, 6, plane)))
                m_one[z + 1, rows, :] = bit(code, 8, one)
                m_two[z + 2, rows, :] = bit(code, 10, two)
                if z == 0:
                    m_one[0, rows, :] = bit(code, 9, one)
                if z < 2:
                    m_two[z, rows, :] = bit(code, 11, two)
                mov[z, rows, :] = (1 - fixed[z, rows, :]).astype(F32)
            out[j] = out[j] + gather_edges(kept, g)
        return tuple(out)

    edge_codes = lax.fori_loop(0, 8, masks, (jnp.zeros((8, 128), jnp.int32),) * 2, unroll=2)
    for j in range(2):
        for n, (first, last) in enumerate(((5, 7), (1, 0), (6, 4))):
            m_edge[n, 8 * j:8 * j + 8, :] = jnp.where(odd8, bit(edge_codes[j], first, plane), bit(edge_codes[j], last, plane))
    for z in range(6):
        code = codes[z, 0:1, :]
        line = lax.broadcasted_iota(jnp.int32, (1, 128), 1)
        m_top[0, z:z + 1, :] = bit(code, 3, plane)
        m_top[1, z:z + 1, :] = jnp.where(line == 127, 0.0, bit(code, 7, plane))
        m_top[2, z:z + 1, :] = jnp.where(line == 0, 0.0, bit(code, 5, plane))

    def build_halo(it, c):
        def got(slot, j):
            return edge_in[it, slot, c, 8 * j:8 * j + 8, :]

        near_rows = [jnp.where(odd8, lanes_right(got(FROM_LEFT, j)), lanes_left(got(FROM_RIGHT, j))) for j in range(2)]
        up = jnp.where(odd8, pltpu.roll(got(FROM_UP_LEFT, 1), 17, 1), pltpu.roll(got(FROM_UP_RIGHT, 1), 15, 1))
        down = jnp.where(odd8, pltpu.roll(got(FROM_DOWN_LEFT, 0), 113, 1), pltpu.roll(got(FROM_DOWN_RIGHT, 0), 111, 1))
        above = jnp.where(group_of == 0, up, pltpu.roll(near_rows[1], 16, 1))
        under = jnp.where(group_of == 7, down, pltpu.roll(near_rows[0], 112, 1))
        return [above, near_rows[0], near_rows[1], under]

    loads[2].wait()
    scale = None
    damp = F32(DAMPING)
    for it in range(ITERS):
        first = it == 0

        def advance(z, carry):
            for i in range(16):
                rows = slice(8 * i, 8 * i + 8)
                for c in range(2):
                    p = pos[c, z, rows, :]
                    if not first:
                        p = p + scale * kick[c, z, rows, :]
                        pos[c, z, rows, :] = p
                    p = lanes_left(p)
                    rolled[c, z, rows, :] = p + 1.0 if c else p
            return carry

        lax.fori_loop(0, 6, advance, 0, unroll=6)

        if first:
            meet(1)
            greet(2)
        if comm and first:
            for n in range(2, 10):
                copies[it][n].wait_recv()

        for c in range(2):
            own, up, down = row_own[it, 0, c], row_in[it, 0, c], row_in[it, 1, c]
            edges = edge_own[it, c]
            halo = build_halo(it, c) if first else [edge_next[c, 8 * n:8 * n + 8, :] for n in range(4)]
            if not first:
                own = row_pos[c] + scale * own
                up = up_pos[c] + scale * up
                down = down_pos[c] + scale * down
                edges = edge_pos[c] + jnp.concatenate([scale, scale], 0) * edges
                halo = [edge_halo[c, 8 * n:8 * n + 8, :] + scale * h for n, h in enumerate(halo)]
            row_pos[c], up_pos[c], down_pos[c], edge_pos[c] = own, up, down, edges
            for n, h in enumerate(halo):
                edge_halo[c, 8 * n:8 * n + 8, :] = h
            right = lanes_left(down)
            right = right + 1.0 if c else right
            for z in range(6):
                pos[c, z, 128:129, :] = down[z:z + 1, :]
                rolled[c, z, 128:129, :] = right[z:z + 1, :]

        top = [zero, zero]
        own_y, own_x, up_y, up_x = row_pos[0], row_pos[1], up_pos[0], up_pos[1]
        for n, (step, turn) in enumerate(((0, 0), (1, 127), (-1, 1))):
            ny_, nx_ = (pltpu.roll(up_y, turn, 1), pltpu.roll(up_x, turn, 1)) if turn else (up_y, up_x)
            dy, dx = ny_ - own_y - 1.0, nx_ - own_x + float(step)
            w = plane_weight(dy, dx, DIAG if step else 1.0, m_top[n])
            top = [top[0] + w * dy, top[1] + w * dx]
        for c in range(2):
            for z in range(6):
                below[c, z, 7:8, :] = -top[c][z:z + 1, :]
                below_right[c, z, 7:8, :] = jnp.zeros((1, 128), F32)

        side = [jnp.zeros((16, 128), F32)] * 2
        way = jnp.where(odd16, F32(-1.0), F32(1.0))
        own_y, own_x = edge_pos[0], edge_pos[1]
        for n, step in enumerate((-1, 0, 1)):
            dy = edge_halo[0, 8 + step:24 + step, :] - own_y + float(step)
            dx = edge_halo[1, 8 + step:24 + step, :] - own_x + way
            w = plane_weight(dy, dx, DIAG if step else 1.0, m_edge[n])
            side = [side[0] + w * dy, side[1] + w * dx]
        for c in range(2):
            edge_force[c] = side[c]

        def in_plane(z, carry):
            for i in range(16):
                r = 8 * i
                rows, next_rows = slice(r, r + 8), slice(r + 1, r + 9)
                y, x = pos[0, z, rows, :], pos[1, z, rows, :]
                y_d, x_d = pos[0, z, next_rows, :], pos[1, z, next_rows, :]
                y_r, x_r = rolled[0, z, rows, :], rolled[1, z, rows, :]
                y_dr, x_dr = rolled[0, z, next_rows, :], rolled[1, z, next_rows, :]
                y_less, y_r_less = y - 1.0, y_r - 1.0

                def link(dy, dx, rest, n):
                    w = plane_weight(dy, dx, rest, m_plane[n, z, rows, :])
                    return w * dy, w * dx

                across = link(y_r - y, x_r - x, 1.0, 0)
                down = link(y_d - y_less, x_d - x, 1.0, 1)
                diag = link(y_dr - y_less, x_dr - x, DIAG, 2)
                anti = link(y_d - y_r_less, x_d - x_r, DIAG, 3)
                for c in range(2):
                    below[c, z, r + 8:r + 16, :] = down[c] + anti[c]
                    below_right[c, z, r + 8:r + 16, :] = diag[c]
                    here = across[c] + down[c] + diag[c] - below[c, z, r + 7:r + 15, :]
                    right = anti[c] - across[c] - below_right[c, z, r + 7:r + 15, :]
                    force[c, z, rows, :] = here + lanes_right(right)
            return carry

        lax.fori_loop(0, 6, in_plane, 0, unroll=2)

        if first:
            meet(2)
        if comm:
            for n in range(2):
                copies[it][n].wait()

        def depth(g, carry):
            energy, packed = carry[0], list(carry[1:])
            for j in range(2):
                r = pl.multiple_of(16 * g + 8 * j, 8)
                rows = pl.ds(r, 8)
                at, got = {}, {}
                for z in range(6):
                    at[z] = [pos[c, z, rows, :] for c in range(2)]
                    got[z] = [force[c, z, rows, :] for c in range(2)]
                for s in range(2):
                    for n in range(2):
                        vals = []
                        for c in range(2):
                            v = z_in[0, s, c, n, rows, :]
                            if not first:
                                v = v + scale * z_in[it, s, c, n, rows, :]
                                if it < ITERS - 1:
                                    z_in[0, s, c, n, rows, :] = v
                            vals.append(v)
                        at[n - 2 if s == 0 else n + 6] = vals
                for reach, mask in ((1, m_one), (2, m_two)):
                    for z in range(-reach, 6):
                        a, b = at[z], at[z + reach]
                        dy, dx = b[0] - a[0], b[1] - a[1]
                        w = depth_weight(dy, dx, mask[z + reach, rows, :])
                        for c, d in enumerate((w * dy, w * dx)):
                            if z >= 0:
                                got[z][c] = got[z][c] + d
                            if z + reach < 6:
                                got[z + reach][c] = got[z + reach][c] - d
                kicked = [[], []]
                for c in range(2):
                    edge = pltpu.roll(edge_force[c, 8 * j:8 * j + 8, :], lax.rem(128 - 16 * g, 128), 1)
                    for z in range(6):
                        f = got[z][c] + jnp.where(is_edge, pltpu.roll(edge, 127 - 2 * z, 1), 0.0)
                        k = (damp * kick[c, z, rows, :] + f) * mov[z, rows, :]
                        kick[c, z, rows, :] = k
                        energy = energy + k * k
                        kicked[c].append(k)
                    if it < ITERS - 1:
                        packed[2 * c + j] = packed[2 * c + j] + gather_edges(kicked[c], g)
            return (energy, *packed)

        energy, *packed = lax.fori_loop(0, 8, depth, (zero,) * 5, unroll=4)

        total = jnp.sum(energy, axis=0, keepdims=True)
        send_sum(it, 0, group_a, sum_a, total)
        if it < ITERS - 1:
            if comm:
                copies.append(halo_copies(it + 1, kick))
                for c in copies[it + 1][:2]:
                    c.start()
            pack_rows(it + 1, kick)
            for c in range(2):
                for j in range(2):
                    edge_own[it + 1, c, 8 * j:8 * j + 8, :] = packed[2 * c + j]
            if comm:
                for c in copies[it + 1][2:]:
                    c.start()
        else:
            outs = [
                pltpu.make_async_copy(pos.at[:, :, pl.ds(0, 128), :], pos_out, out_sem.at[0]),
                pltpu.make_async_copy(kick, kick_out, out_sem.at[1]),
            ]
            for c in outs:
                c.start()
        total = take_sum(it, 0, group_a, sum_a, total)
        send_sum(it, 1, group_b, sum_b, total)
        if it < ITERS - 1:
            if comm:
                for n in range(2, 10):
                    copies[it + 1][n].wait_recv()
            for c in range(2):
                for n, h in enumerate(build_halo(it + 1, c)):
                    edge_next[c, 8 * n:8 * n + 8, :] = h
        else:
            for c in outs:
                c.wait()
        total = take_sum(it, 1, group_b, sum_b, total)
        kinetic = 0.5 * jnp.sum(total, axis=1, keepdims=True)
        factor = jnp.minimum(1.0, jnp.sqrt(ENERGY_CAP * nodes_all / (kinetic + EPSILON)))
        factor = jnp.broadcast_to(factor, (8, 128))
        scale = TIME_STEP * factor
        damp = DAMPING * factor

    fac_out[...] = factor
    if comm:
        for it in range(ITERS):
            for c in copies[it][2:]:
                c.wait_send()
            wait_sums_sent(it)


def local(sizes, comm, positions, velocities, link_codes, fixed_nodes):
    nx, ny, nz = sizes
    _, deep, rows, cols = positions.shape
    assert (deep, rows, cols) == (6, 128, 128)
    nodes_all = deep * rows * cols * nx * ny * nz
    vmem = pltpu.VMEM
    block = (2, 6, 128, 128)
    scratch = [
        vmem((2, 6, 136, 128), F32),
        vmem((2, 6, 136, 128), F32),
        vmem(block, F32),
        vmem(block, F32),
        vmem((2, 6, 136, 128), F32),
        vmem((2, 6, 136, 128), F32),
        vmem((6, 128, 128), jnp.int32),
        vmem((6, 128, 128), jnp.int32),
        vmem((4, 6, 128, 128), F32),
        vmem((7, 128, 128), F32),
        vmem((8, 128, 128), F32),
        vmem((6, 128, 128), F32),
        vmem((ITERS, 2, 2, 2, 128, 128), F32),
        vmem((ITERS, 2, 16, 128), F32),
        vmem((ITERS, 6, 2, 16, 128), F32),
        vmem((ITERS, 2, 2, 8, 128), F32),
        vmem((ITERS, 2, 2, 8, 128), F32),
        vmem((2, 16, 128), F32),
        vmem((2, 32, 128), F32),
        vmem((2, 8, 128), F32),
        vmem((2, 8, 128), F32),
        vmem((2, 8, 128), F32),
        vmem((3, 16, 128), F32),
        vmem((3, 8, 128), F32),
        vmem((2, 16, 128), F32),
        vmem((2, 32, 128), F32),
        vmem((ITERS, 2, 1, 128), F32),
        vmem((ITERS, ny, 1, 128), F32),
        vmem((ITERS, nx * nz, 1, 128), F32),
        pltpu.SemaphoreType.DMA((4,)),
        pltpu.SemaphoreType.DMA((2,)),
        pltpu.SemaphoreType.DMA((ITERS, 10)),
        pltpu.SemaphoreType.DMA((ITERS, 10)),
        pltpu.SemaphoreType.DMA((ITERS, 2)),
        pltpu.SemaphoreType.DMA((ITERS, 2)),
        pltpu.SemaphoreType.REGULAR((3,)),
    ]
    anywhere = pl.BlockSpec(memory_space=pltpu.MemorySpace.HBM)
    position, kicked, factor = pl.pallas_call(
        functools.partial(kernel, (nx, ny, nz, nodes_all), comm),
        out_shape=(
            pltpu.VMEM(block, F32),
            pltpu.VMEM(block, F32),
            pltpu.VMEM((8, 128), F32),
        ),
        in_specs=[anywhere] * 4,
        out_specs=(pl.BlockSpec(memory_space=pltpu.VMEM),) * 3,
        scratch_shapes=scratch,
        compiler_params=pltpu.CompilerParams(
            collective_id=0 if comm else None, has_side_effects=True, vmem_limit_bytes=32 * 1024 * 1024),
    )(*(pltpu.with_memory_space_constraint(a, pltpu.HBM) for a in (positions, velocities, link_codes, fixed_nodes)))
    tiles = (2, deep, rows // 8, 8, cols)
    velocity = factor * kicked.reshape(tiles)
    position = position.reshape(tiles) + TIME_STEP * velocity
    return (position.reshape(block), velocity.reshape(block))


def solution(mesh, comm=True):
    sizes = tuple(mesh.shape[a] for a in AXES)
    in_specs = (
        P(None, "gz", "gy", "gx"),
        P(None, "gz", "gy", "gx"),
        P("gz", "gy", "gx"),
        P("gz", "gy", "gx"),
    )
    out_specs = (P(None, "gz", "gy", "gx"), P(None, "gz", "gy", "gx"))
    return jax.shard_map(
        functools.partial(local, sizes, comm), mesh=mesh, in_specs=in_specs, out_specs=out_specs, check_vma=False)
```

```python
import functools
import itertools
import math

import jax
import jax.numpy as jnp
from jax import lax
from jax.experimental import pallas as pl
from jax.experimental.pallas import tpu as pltpu
from jax.sharding import PartitionSpec as P

MESH = pl.DeviceIdType.MESH
ITERS = 3
TIME_STEP = 0.3
DAMPING = 0.9
STIFF_PLANE = 1.0
HUBER_DELTA = 0.5
LENGTH_FLOOR = 0.25
ENERGY_CAP = 0.04
EPSILON = 1e-06
DIAG = math.sqrt(2.0)
AXES = ("gx", "gy", "gz")
F32 = jnp.float32

COLUMN_PEERS = ((1, 0), (-1, 0), (1, 1), (-1, 1), (1, -1), (-1, -1))
FROM_LEFT, FROM_RIGHT, FROM_UP_LEFT, FROM_UP_RIGHT, FROM_DOWN_LEFT, FROM_DOWN_RIGHT = range(6)


def lanes_left(a):
    return pltpu.roll(a, 127, 1)


def lanes_right(a):
    return pltpu.roll(a, 1, 1)


def plane_weight(dy, dx, rest, mask):
    square = dy * dy + dx * dx
    u = jnp.minimum(lax.rsqrt(square), 1.0 / LENGTH_FLOOR)
    stretch = jnp.clip(square * u - rest, -HUBER_DELTA, HUBER_DELTA)
    return stretch * u * mask


def depth_weight(dy, dx, mask):
    square = dy * dy + dx * dx
    return jnp.minimum(lax.rsqrt(square), 1.0 / HUBER_DELTA) * mask


def bit(codes, index, scale):
    return jnp.where((codes & (1 << index)) != 0, F32(scale), F32(0.0))


def kernel(sizes, comm, *refs):
    (pos_in, vel_in, code_in, fix_in, pos_out, kick_out, fac_out,
     pos, rolled, kick, force, below, below_right, codes, fixed, m_plane, m_one, m_two, mov,
     z_in, edge_own, edge_in, row_own, row_in, edge_pos, edge_halo, row_pos, up_pos, down_pos,
     m_edge, m_top, edge_force, edge_next, sum_src, sum_a, sum_b,
     load_sem, out_sem, halo_send, halo_recv, sum_send, sum_recv, greeted) = refs
    nx, ny, nz, nodes_all = sizes
    chips = ny // 2
    me = {a: lax.axis_index(a) for a in AXES}

    def shifted(ox, oy, oz):
        return (lax.rem(me["gx"] + ox + nx, nx), lax.rem(me["gy"] + oy + ny, ny), lax.rem(me["gz"] + oz + nz, nz))

    def by_chip(ox, chip, core, oz):
        gy = me["gy"]
        where = lax.rem(lax.div(gy, 2) + chip, chips) * 2 + lax.rem(lax.rem(gy, 2) + core, 2)
        return (lax.rem(me["gx"] + ox, nx), where, lax.rem(me["gz"] + oz, nz))

    def far(o):
        ox, chip, core, oz = o
        return -(min(ox, nx - ox) + min(chip, chips - chip) + min(oz, nz - oz)) - 0.1 * core

    group_a = sorted([(0, c, k, 0) for c in range(chips) for k in range(2) if c or k], key=far)
    group_b = sorted([(i, 0, 0, k) for i in range(nx) for k in range(nz) if i or k], key=far)

    loads = [
        pltpu.make_async_copy(pos_in, pos.at[:, :, pl.ds(0, 128), :], load_sem.at[0]),
        pltpu.make_async_copy(code_in, codes, load_sem.at[1]),
        pltpu.make_async_copy(vel_in, kick, load_sem.at[2]),
        pltpu.make_async_copy(fix_in, fixed, load_sem.at[3]),
    ]
    for c in loads:
        c.start()

    if comm:
        barrier = pltpu.get_barrier_semaphore()
        beside = [(1, 0, 0, 0), (nx - 1, 0, 0, 0), (0, 0, 0, 1), (0, 0, 0, nz - 1),
                  (0, 1, 0, 0), (0, chips - 1, 0, 0), (0, 0, 1, 0)]
        peers = [shifted(i, j, 0) for i in (1, -1, 0) for j in (1, -1)] + [by_chip(*o) for o in beside]
        for peer in peers:
            pl.semaphore_signal(barrier, inc=1, device_id=peer, device_id_type=MESH)
    rounds = [
        [(1, 0, 0, 0), (nx - 1, 0, 0, 0), (0, 0, 0, 1), (0, 0, 0, nz - 1), (0, 1, 0, 0), (0, chips - 1, 0, 0), (0, 0, 1, 0)],
        [(2, 0, 0, 0), (nx - 2, 0, 0, 0), (0, 0, 0, 2), (0, 0, 0, nz - 2), (0, 0, 1, 0)],
        [(0, 0, 0, k) for k in range(1, nz)],
    ]

    def greet(n):
        if comm:
            for o in rounds[n]:
                pl.semaphore_signal(greeted.at[n], inc=1, device_id=by_chip(*o), device_id_type=MESH)

    def meet(n):
        if comm:
            pl.semaphore_wait(greeted.at[n], len(rounds[n]))

    lane = lax.broadcasted_iota(jnp.int32, (8, 128), 1)
    is_last = lane == 127
    is_first = lane == 0
    is_edge = is_last | is_first
    pair = [(lane >> 1) == z for z in range(6)]
    odd16 = (lax.broadcasted_iota(jnp.int32, (16, 128), 1) & 1) == 1
    odd8 = (lane & 1) == 1
    group_of = lane >> 4
    zero = jnp.zeros((8, 128), F32)

    def gather_edges(values, g):
        packed = jnp.zeros_like(values[0])
        for z in range(6):
            packed = jnp.where(pair[z], pltpu.roll(values[z], 2 * z + 1, 1), packed)
        return pltpu.roll(packed, 16 * g, 1)

    def pack_rows(it, source):
        for c in range(2):
            for z in range(6):
                row_own[it, 0, c, z:z + 1, :] = source[c, z, 0:1, :]
                row_own[it, 1, c, z:z + 1, :] = source[c, z, 127:128, :]

    def halo_copies(it, source):
        out = []
        for side, (oz, first) in enumerate(((1, 4), (-1, 0))):
            out.append((source.at[:, pl.ds(first, 2), pl.ds(0, 128), :], z_in.at[it, side], shifted(0, 0, oz)))
        for side, (oy, which) in enumerate(((1, 1), (-1, 0))):
            out.append((row_own.at[it, which], row_in.at[it, side], shifted(0, oy, 0)))
        for slot, (ox, oy) in enumerate(COLUMN_PEERS):
            part = pl.ds(0, 16) if oy == 0 else pl.ds(8 if oy == 1 else 0, 8)
            out.append((edge_own.at[it, :, part, :], edge_in.at[it, slot, :, part, :], shifted(ox, oy, 0)))
        return [
            pltpu.make_async_remote_copy(
                src_ref=s, dst_ref=d, send_sem=halo_send.at[it, n], recv_sem=halo_recv.at[it, n],
                device_id=peer, device_id_type=MESH)
            for n, (s, d, peer) in enumerate(out)
        ]

    def send_sum(it, phase, group, buffer, value):
        if not comm:
            return
        sum_src[it, phase] = value
        for k, o in enumerate(group, 1):
            pltpu.make_async_remote_copy(
                src_ref=sum_src.at[it, phase], dst_ref=buffer.at[it, k],
                send_sem=sum_send.at[it, phase], recv_sem=sum_recv.at[it, phase],
                device_id=by_chip(*o), device_id_type=MESH).start()

    def take_sum(it, phase, group, buffer, value):
        if not comm:
            return value
        got = buffer.at[it, pl.ds(1, len(group))]
        pltpu.make_async_remote_copy(
            src_ref=got, dst_ref=got, send_sem=sum_send.at[it, phase], recv_sem=sum_recv.at[it, phase],
            device_id=by_chip(*group[0]), device_id_type=MESH).wait_recv()
        terms = [value] + [buffer[it, k] for k in range(1, len(group) + 1)]
        while len(terms) > 1:
            terms = [a + b for a, b in zip(terms[::2], terms[1::2])] + (terms[-1:] if len(terms) % 2 else [])
        return terms[0]

    def wait_sums_sent(it):
        for phase, (group, buffer) in enumerate(((group_a, sum_a), (group_b, sum_b))):
            got = buffer.at[it, pl.ds(1, len(group))]
            pltpu.make_async_remote_copy(
                src_ref=got, dst_ref=got, send_sem=sum_send.at[it, phase], recv_sem=sum_recv.at[it, phase],
                device_id=by_chip(*group[0]), device_id_type=MESH).wait_send()

    row_own[...] = jnp.zeros_like(row_own)
    loads[0].wait()
    if comm:
        pl.semaphore_wait(barrier, len(peers))
        copies = [halo_copies(0, pos)]
        for c in copies[0][:2]:
            c.start()
    greet(0)
    pack_rows(0, pos)

    def pack_positions(g, packed):
        out = list(packed)
        for j in range(2):
            r = pl.multiple_of(16 * g + 8 * j, 8)
            for c in range(2):
                values = [pos[c, z, pl.ds(r, 8), :] for z in range(6)]
                out[2 * c + j] = out[2 * c + j] + gather_edges(values, g)
        return tuple(out)

    packed = lax.fori_loop(0, 8, pack_positions, (zero,) * 4, unroll=4)
    for c in range(2):
        for j in range(2):
            edge_own[0, c, 8 * j:8 * j + 8, :] = packed[2 * c + j]

    if comm:
        for c in copies[0][2:]:
            c.start()
    meet(0)
    greet(1)

    loads[1].wait()
    loads[3].wait()
    plane = TIME_STEP * STIFF_PLANE
    one = TIME_STEP * HUBER_DELTA * 0.5
    two = TIME_STEP * HUBER_DELTA * 0.25

    def masks(g, packed):
        out = list(packed)
        for j in range(2):
            r = pl.multiple_of(16 * g + 8 * j, 8)
            rows = pl.ds(r, 8)
            kept = []
            for z in range(6):
                code = codes[z, rows, :]
                kept.append(code)
                m_plane[0, z, rows, :] = jnp.where(is_last, 0.0, bit(code, 0, plane))
                m_plane[1, z, rows, :] = bit(code, 2, plane)
                m_plane[2, z, rows, :] = jnp.where(is_last, 0.0, bit(code, 4, plane))
                m_plane[3, z, rows, :] = jnp.where(is_last, 0.0, lanes_left(bit(code, 6, plane)))
                m_one[z + 1, rows, :] = bit(code, 8, one)
                m_two[z + 2, rows, :] = bit(code, 10, two)
                if z == 0:
                    m_one[0, rows, :] = bit(code, 9, one)
                if z < 2:
                    m_two[z, rows, :] = bit(code, 11, two)
                mov[z, rows, :] = (1 - fixed[z, rows, :]).astype(F32)
            out[j] = out[j] + gather_edges(kept, g)
        return tuple(out)

    edge_codes = lax.fori_loop(0, 8, masks, (jnp.zeros((8, 128), jnp.int32),) * 2, unroll=4)
    for j in range(2):
        for n, (first, last) in enumerate(((5, 7), (1, 0), (6, 4))):
            m_edge[n, 8 * j:8 * j + 8, :] = jnp.where(odd8, bit(edge_codes[j], first, plane), bit(edge_codes[j], last, plane))
    for z in range(6):
        code = codes[z, 0:1, :]
        line = lax.broadcasted_iota(jnp.int32, (1, 128), 1)
        m_top[0, z:z + 1, :] = bit(code, 3, plane)
        m_top[1, z:z + 1, :] = jnp.where(line == 127, 0.0, bit(code, 7, plane))
        m_top[2, z:z + 1, :] = jnp.where(line == 0, 0.0, bit(code, 5, plane))

    def build_halo(it, c):
        def got(slot, j):
            return edge_in[it, slot, c, 8 * j:8 * j + 8, :]

        near_rows = [jnp.where(odd8, lanes_right(got(FROM_LEFT, j)), lanes_left(got(FROM_RIGHT, j))) for j in range(2)]
        up = jnp.where(odd8, pltpu.roll(got(FROM_UP_LEFT, 1), 17, 1), pltpu.roll(got(FROM_UP_RIGHT, 1), 15, 1))
        down = jnp.where(odd8, pltpu.roll(got(FROM_DOWN_LEFT, 0), 113, 1), pltpu.roll(got(FROM_DOWN_RIGHT, 0), 111, 1))
        above = jnp.where(group_of == 0, up, pltpu.roll(near_rows[1], 16, 1))
        under = jnp.where(group_of == 7, down, pltpu.roll(near_rows[0], 112, 1))
        return [above, near_rows[0], near_rows[1], under]

    loads[2].wait()
    scale = None
    damp = F32(DAMPING)
    for it in range(ITERS):
        first = it == 0

        def advance(z, carry):
            for i in range(16):
                rows = slice(8 * i, 8 * i + 8)
                for c in range(2):
                    p = pos[c, z, rows, :]
                    if not first:
                        p = p + scale * kick[c, z, rows, :]
                        pos[c, z, rows, :] = p
                    p = lanes_left(p)
                    rolled[c, z, rows, :] = p + 1.0 if c else p
            return carry

        lax.fori_loop(0, 6, advance, 0, unroll=6)

        if first:
            meet(1)
            greet(2)
        if comm and first:
            for n in range(2, 10):
                copies[it][n].wait_recv()

        for c in range(2):
            own, up, down = row_own[it, 0, c], row_in[it, 0, c], row_in[it, 1, c]
            edges = edge_own[it, c]
            halo = build_halo(it, c) if first else [edge_next[c, 8 * n:8 * n + 8, :] for n in range(4)]
            if not first:
                own = row_pos[c] + scale * own
                up = up_pos[c] + scale * up
                down = down_pos[c] + scale * down
                edges = edge_pos[c] + jnp.concatenate([scale, scale], 0) * edges
                halo = [edge_halo[c, 8 * n:8 * n + 8, :] + scale * h for n, h in enumerate(halo)]
            row_pos[c], up_pos[c], down_pos[c], edge_pos[c] = own, up, down, edges
            for n, h in enumerate(halo):
                edge_halo[c, 8 * n:8 * n + 8, :] = h
            right = lanes_left(down)
            right = right + 1.0 if c else right
            for z in range(6):
                pos[c, z, 128:129, :] = down[z:z + 1, :]
                rolled[c, z, 128:129, :] = right[z:z + 1, :]

        top = [zero, zero]
        own_y, own_x, up_y, up_x = row_pos[0], row_pos[1], up_pos[0], up_pos[1]
        for n, (step, turn) in enumerate(((0, 0), (1, 127), (-1, 1))):
            ny_, nx_ = (pltpu.roll(up_y, turn, 1), pltpu.roll(up_x, turn, 1)) if turn else (up_y, up_x)
            dy, dx = ny_ - own_y - 1.0, nx_ - own_x + float(step)
            w = plane_weight(dy, dx, DIAG if step else 1.0, m_top[n])
            top = [top[0] + w * dy, top[1] + w * dx]
        for c in range(2):
            for z in range(6):
                below[c, z, 7:8, :] = -top[c][z:z + 1, :]
                below_right[c, z, 7:8, :] = jnp.zeros((1, 128), F32)

        side = [jnp.zeros((16, 128), F32)] * 2
        way = jnp.where(odd16, F32(-1.0), F32(1.0))
        own_y, own_x = edge_pos[0], edge_pos[1]
        for n, step in enumerate((-1, 0, 1)):
            dy = edge_halo[0, 8 + step:24 + step, :] - own_y + float(step)
            dx = edge_halo[1, 8 + step:24 + step, :] - own_x + way
            w = plane_weight(dy, dx, DIAG if step else 1.0, m_edge[n])
            side = [side[0] + w * dy, side[1] + w * dx]
        for c in range(2):
            edge_force[c] = side[c]

        def in_plane(z, carry):
            for i in range(16):
                r = 8 * i
                rows, next_rows = slice(r, r + 8), slice(r + 1, r + 9)
                y, x = pos[0, z, rows, :], pos[1, z, rows, :]
                y_d, x_d = pos[0, z, next_rows, :], pos[1, z, next_rows, :]
                y_r, x_r = rolled[0, z, rows, :], rolled[1, z, rows, :]
                y_dr, x_dr = rolled[0, z, next_rows, :], rolled[1, z, next_rows, :]
                y_less, y_r_less = y - 1.0, y_r - 1.0

                def link(dy, dx, rest, n):
                    w = plane_weight(dy, dx, rest, m_plane[n, z, rows, :])
                    return w * dy, w * dx

                across = link(y_r - y, x_r - x, 1.0, 0)
                down = link(y_d - y_less, x_d - x, 1.0, 1)
                diag = link(y_dr - y_less, x_dr - x, DIAG, 2)
                anti = link(y_d - y_r_less, x_d - x_r, DIAG, 3)
                for c in range(2):
                    below[c, z, r + 8:r + 16, :] = down[c] + anti[c]
                    below_right[c, z, r + 8:r + 16, :] = diag[c]
                    here = across[c] + down[c] + diag[c] - below[c, z, r + 7:r + 15, :]
                    right = anti[c] - across[c] - below_right[c, z, r + 7:r + 15, :]
                    force[c, z, rows, :] = here + lanes_right(right)
            return carry

        lax.fori_loop(0, 6, in_plane, 0, unroll=2)

        if first:
            meet(2)
        if comm:
            for n in range(2):
                copies[it][n].wait()

        def depth(g, carry):
            energy, packed = carry[0], list(carry[1:])
            for j in range(2):
                r = pl.multiple_of(16 * g + 8 * j, 8)
                rows = pl.ds(r, 8)
                at, got = {}, {}
                for z in range(6):
                    at[z] = [pos[c, z, rows, :] for c in range(2)]
                    got[z] = [force[c, z, rows, :] for c in range(2)]
                for s in range(2):
                    for n in range(2):
                        vals = []
                        for c in range(2):
                            v = z_in[0, s, c, n, rows, :]
                            if not first:
                                v = v + scale * z_in[it, s, c, n, rows, :]
                                if it < ITERS - 1:
                                    z_in[0, s, c, n, rows, :] = v
                            vals.append(v)
                        at[n - 2 if s == 0 else n + 6] = vals
                for reach, mask in ((1, m_one), (2, m_two)):
                    for z in range(-reach, 6):
                        a, b = at[z], at[z + reach]
                        dy, dx = b[0] - a[0], b[1] - a[1]
                        w = depth_weight(dy, dx, mask[z + reach, rows, :])
                        for c, d in enumerate((w * dy, w * dx)):
                            if z >= 0:
                                got[z][c] = got[z][c] + d
                            if z + reach < 6:
                                got[z + reach][c] = got[z + reach][c] - d
                kicked = [[], []]
                for c in range(2):
                    edge = pltpu.roll(edge_force[c, 8 * j:8 * j + 8, :], lax.rem(128 - 16 * g, 128), 1)
                    for z in range(6):
                        f = got[z][c] + jnp.where(is_edge, pltpu.roll(edge, 127 - 2 * z, 1), 0.0)
                        k = (damp * kick[c, z, rows, :] + f) * mov[z, rows, :]
                        kick[c, z, rows, :] = k
                        energy = energy + k * k
                        kicked[c].append(k)
                    if it < ITERS - 1:
                        packed[2 * c + j] = packed[2 * c + j] + gather_edges(kicked[c], g)
            return (energy, *packed)

        energy, *packed = lax.fori_loop(0, 8, depth, (zero,) * 5, unroll=4)

        total = jnp.sum(energy, axis=0, keepdims=True)
        send_sum(it, 0, group_a, sum_a, total)
        if it < ITERS - 1:
            if comm:
                copies.append(halo_copies(it + 1, kick))
                for c in copies[it + 1][:2]:
                    c.start()
            pack_rows(it + 1, kick)
            for c in range(2):
                for j in range(2):
                    edge_own[it + 1, c, 8 * j:8 * j + 8, :] = packed[2 * c + j]
            if comm:
                for c in copies[it + 1][2:]:
                    c.start()
        else:
            outs = [
                pltpu.make_async_copy(pos.at[:, :, pl.ds(0, 128), :], pos_out, out_sem.at[0]),
                pltpu.make_async_copy(kick, kick_out, out_sem.at[1]),
            ]
            for c in outs:
                c.start()
        total = take_sum(it, 0, group_a, sum_a, total)
        send_sum(it, 1, group_b, sum_b, total)
        if it < ITERS - 1:
            if comm:
                for n in range(2, 10):
                    copies[it + 1][n].wait_recv()
            for c in range(2):
                for n, h in enumerate(build_halo(it + 1, c)):
                    edge_next[c, 8 * n:8 * n + 8, :] = h
        else:
            for c in outs:
                c.wait()
        total = take_sum(it, 1, group_b, sum_b, total)
        kinetic = 0.5 * jnp.sum(total, axis=1, keepdims=True)
        factor = jnp.minimum(1.0, jnp.sqrt(ENERGY_CAP * nodes_all / (kinetic + EPSILON)))
        factor = jnp.broadcast_to(factor, (8, 128))
        scale = TIME_STEP * factor
        damp = DAMPING * factor

    fac_out[...] = factor
    if comm:
        for it in range(ITERS):
            for c in copies[it][2:]:
                c.wait_send()
            wait_sums_sent(it)


def local(sizes, comm, positions, velocities, link_codes, fixed_nodes):
    nx, ny, nz = sizes
    _, deep, rows, cols = positions.shape
    assert (deep, rows, cols) == (6, 128, 128)
    nodes_all = deep * rows * cols * nx * ny * nz
    vmem = pltpu.VMEM
    block = (2, 6, 128, 128)
    scratch = [
        vmem((2, 6, 136, 128), F32),
        vmem((2, 6, 136, 128), F32),
        vmem(block, F32),
        vmem(block, F32),
        vmem((2, 6, 136, 128), F32),
        vmem((2, 6, 136, 128), F32),
        vmem((6, 128, 128), jnp.int32),
        vmem((6, 128, 128), jnp.int32),
        vmem((4, 6, 128, 128), F32),
        vmem((7, 128, 128), F32),
        vmem((8, 128, 128), F32),
        vmem((6, 128, 128), F32),
        vmem((ITERS, 2, 2, 2, 128, 128), F32),
        vmem((ITERS, 2, 16, 128), F32),
        vmem((ITERS, 6, 2, 16, 128), F32),
        vmem((ITERS, 2, 2, 8, 128), F32),
        vmem((ITERS, 2, 2, 8, 128), F32),
        vmem((2, 16, 128), F32),
        vmem((2, 32, 128), F32),
        vmem((2, 8, 128), F32),
        vmem((2, 8, 128), F32),
        vmem((2, 8, 128), F32),
        vmem((3, 16, 128), F32),
        vmem((3, 8, 128), F32),
        vmem((2, 16, 128), F32),
        vmem((2, 32, 128), F32),
        vmem((ITERS, 2, 1, 128), F32),
        vmem((ITERS, ny, 1, 128), F32),
        vmem((ITERS, nx * nz, 1, 128), F32),
        pltpu.SemaphoreType.DMA((4,)),
        pltpu.SemaphoreType.DMA((2,)),
        pltpu.SemaphoreType.DMA((ITERS, 10)),
        pltpu.SemaphoreType.DMA((ITERS, 10)),
        pltpu.SemaphoreType.DMA((ITERS, 2)),
        pltpu.SemaphoreType.DMA((ITERS, 2)),
        pltpu.SemaphoreType.REGULAR((3,)),
    ]
    anywhere = pl.BlockSpec(memory_space=pltpu.MemorySpace.HBM)
    position, kicked, factor = pl.pallas_call(
        functools.partial(kernel, (nx, ny, nz, nodes_all), comm),
        out_shape=(
            pltpu.VMEM(block, F32),
            pltpu.VMEM(block, F32),
            pltpu.VMEM((8, 128), F32),
        ),
        in_specs=[anywhere] * 4,
        out_specs=(pl.BlockSpec(memory_space=pltpu.VMEM),) * 3,
        scratch_shapes=scratch,
        compiler_params=pltpu.CompilerParams(
            collective_id=0 if comm else None, has_side_effects=True, vmem_limit_bytes=32 * 1024 * 1024),
    )(*(pltpu.with_memory_space_constraint(a, pltpu.HBM) for a in (positions, velocities, link_codes, fixed_nodes)))
    tiles = (2, deep, rows // 8, 8, cols)
    velocity = factor * kicked.reshape(tiles)
    position = position.reshape(tiles) + TIME_STEP * velocity
    return (position.reshape(block), velocity.reshape(block))


def solution(mesh, comm=True):
    sizes = tuple(mesh.shape[a] for a in AXES)
    in_specs = (
        P(None, "gz", "gy", "gx"),
        P(None, "gz", "gy", "gx"),
        P("gz", "gy", "gx"),
        P("gz", "gy", "gx"),
    )
    out_specs = (P(None, "gz", "gy", "gx"), P(None, "gz", "gy", "gx"))
    return jax.shard_map(
        functools.partial(local, sizes, comm), mesh=mesh, in_specs=in_specs, out_specs=out_specs, check_vma=False)
```
